128 devices in a mesh: ax: 8 (over z, core), xs: 16 (over x, y).
Axes of the slice: x: 4, y: 4, z: 4, core: 2. Of those that a mesh axis runs over, the one named last changes fastest.
Arguments:
- flow_vector: bfloat16 [3, 16, 64, 32, 512], P(None, 'ax', 'xs'), may hold values from -6 to 6
- thermal_state: bfloat16 [16, 64, 32, 512], P('ax', 'xs'), may hold values from 0.5 to 1.5
- stiffness_weights: float32 [3, 16, 64, 32, 512], P(None, 'ax', 'xs'), may hold values from 0.002 to 0.02
- inertia_over_timestep: float32 [16, 64, 32, 512], P('ax', 'xs'), may hold values from 0.1 to 1
- tracer_interval_index: int32 [3, 524288], P(None, ('ax', 'xs')), may hold values from 0 to 6
- tracer_interval_offset: float32 [3, 524288], P(None, ('ax', 'xs')), may hold values from 0 to 1
- tracer_holding_chip: int32 [524288, 1], P(('ax', 'xs')), may hold values from 0 to 127; in each aligned block of 4096 rows (0 to 4095, 4096 to 8191, ...) at most 128 rows name the same one
- tracer_containing_piece: int32 [524288], P(('ax', 'xs')), may hold values from 0 to 255
- chemical_shares: float32 [6, 524288], P(None, ('ax', 'xs')), may hold values from 0.2 to 1
- frequency_scale: float32 [6], replicated, may hold values from 0.5 to 2
- energy_barrier: float32 [6], replicated, may hold values from 0.5 to 2
Outputs:
- velocity_out: float32 [3, 16, 64, 32, 512], P(None, 'ax', 'xs')
- coords_new: float32 [3, 524288], P(None, ('ax', 'xs'))
- species_new: float32 [6, 524288], P(None, ('ax', 'xs'))
The draws below stay inside these ranges and needn't reach their ends.
Inputs may be any that keep to these rules, and one draw needn't show every extreme that they name: `tracer_holding_chip`: among the particles of one device, at most 128 name the same owner device, and this bound is reached.
All inputs are finite; a program needn't handle non-finite values.
Results may differ from the reference program's by a relative error of at most 0.0003.
Values sent between devices are 32-bit elements; how exact they have to be, the bound alone decides.
A program may use at most 128 MiB of HBM per device.

```python
import math
import jax
import jax.numpy as jnp
import numpy as np
from jax import lax

LOBATTO_COUNT = 8
LENGTHWISE_CHIP = 2
SECTORS_CHIP = 4
DEPTHWISE_COUNT = 32
P_DEV = 4096
LENGTHWISE_ALL = 16
SECTORS_ALL = 64
PIECES_ON_CHIP = 256
PARTS_SIZE = 524288
CAP = 128
N_AX = 8
N_XS = 16
DEVICES = 128


def place_ends(values, stream_key, least, high):
    longest = values.shape.index(max(values.shape))
    spots = []
    for shift in (0, 1):
        where = [jax.random.randint(jax.random.fold_in(stream_key, axis), (), 0, length) for axis, length in enumerate(values.shape)]
        where[longest] = (where[longest] + shift) % values.shape[longest]
        spots.append(tuple(where))
    return values.at[spots[0]].set(least).at[spots[1]].set(high)


def block_levels(key, extent, pieces, low, high):
    level = 1.0
    for axis_at, shards_of in pieces:
        heights = jax.random.uniform(jax.random.fold_in(jax.random.fold_in(key, 6), axis_at), (shards_of,), jnp.float32, low / len(pieces), high / len(pieces))
        level = level * jnp.repeat(jnp.exp(heights), extent[axis_at] // shards_of).reshape((-1,) + (1,) * (len(extent) - 1 - axis_at))
    return level


def shared_out(rng, own, number, rows, number_of, top, limit, lean):
    sequence = jax.random.permutation(rng, number_of)
    crowded, usual = shares(number_of, rows * top, limit, lean, True), shares(number_of, rows * top, limit, lean, False)
    places = jnp.arange(number_of)

    def named(sizes, rotation):
        used = int((sizes > 0).sum())
        fixed = max(1, used // 4)
        passed = fixed + (places - fixed + rotation * (used - fixed)) % max(1, number_of - fixed)
        return jnp.zeros((number_of,), jnp.int32).at[sequence[jnp.where(places < fixed, places, passed)]].set(jnp.asarray(sizes, jnp.int32))

    sizes = jnp.where(number % 4 == 0, named(crowded, number // 4), named(usual, number - number // 4 - 1))
    mixed = jax.random.permutation(jax.random.fold_in(own, 3), number_of)
    donor, taker = mixed[0:number_of // 2 * 2:2], mixed[1:number_of // 2 * 2:2]
    margin = jnp.minimum(sizes[donor] - 1, limit - sizes[taker]) // 2
    margin = jnp.where((donor == sequence[0]) | (taker == sequence[0]) | (sizes[taker] == 0), 0, jnp.maximum(margin, 0))
    passed = jax.random.randint(jax.random.fold_in(own, 4), (number_of // 2,), 0, 1 << 20) % (margin + 1)
    sizes = sizes.at[donor].add(-passed).at[taker].add(passed)
    labels = jnp.searchsorted(jnp.cumsum(sizes), jnp.arange(rows * top), side="right").astype(jnp.int32)
    table = labels.reshape(top, rows).T
    table = table[jax.random.permutation(jax.random.fold_in(own, 1), rows)]
    rotation = jax.random.randint(jax.random.fold_in(own, 2), (rows, 1), 0, top)
    return jnp.take_along_axis(table, (jnp.arange(top)[None, :] + rotation) % top, axis=1)


def shares(amount, total, most, lean, full):
    loads = [(1 << 20) // math.isqrt(standing ** lean) + 1 for standing in range(1, amount + 1)]
    largest = most if full else min(most, max(-(-total // amount), total * loads[0] // sum(loads)))
    least = 1 if total - largest >= amount - 1 else 0
    given, spare = [largest] + [least] * (amount - 1), total - largest - least * (amount - 1)
    while spare > 0:
        movable = [i for i in range(1, amount) if given[i] < largest] or [i for i in range(1, amount) if given[i] < most]
        mass, remaining = sum([loads[i] for i in movable]), spare
        for i in movable:
            addition = min(most - given[i], max(1, remaining * loads[i] // mass), spare)
            given[i] = given[i] + addition
            spare = spare - addition
    return np.array(given)


def scatter_about(stream_key, extent, spread, reach, pieces=(), held_as=jnp.bfloat16):
    gain = block_levels(stream_key, extent, pieces, -0.22, 0.18) if pieces else 1.0
    values = jax.random.normal(stream_key, extent, jnp.float32) * spread * gain
    return jnp.minimum(jnp.maximum(values, -reach), reach).astype(held_as)


def setup_inputs(seed: int = 0) -> dict:
    arg_keys = jax.random.split(jax.random.key(seed), 12)
    flow_vector = scatter_about(arg_keys[0], (3, LENGTHWISE_ALL, SECTORS_ALL, DEPTHWISE_COUNT, LOBATTO_COUNT * LOBATTO_COUNT * LOBATTO_COUNT), 1.0, 6.0, ((1, 8), (2, 16)))
    thermal_state = jnp.clip(0.5 + 1.0 * jax.random.uniform(arg_keys[1], (LENGTHWISE_ALL, SECTORS_ALL, DEPTHWISE_COUNT, LOBATTO_COUNT * LOBATTO_COUNT * LOBATTO_COUNT), jnp.float32) ** block_levels(arg_keys[1], (LENGTHWISE_ALL, SECTORS_ALL, DEPTHWISE_COUNT, LOBATTO_COUNT * LOBATTO_COUNT * LOBATTO_COUNT), ((0, 8), (1, 16)), -0.2, 0.2), 0.5, 1.5).astype(jnp.bfloat16)
    stiffness_weights = jnp.clip(jnp.exp(math.log(0.02) - 2.30258502 * jax.random.uniform(arg_keys[2], (3, LENGTHWISE_ALL, SECTORS_ALL, DEPTHWISE_COUNT, LOBATTO_COUNT * LOBATTO_COUNT * LOBATTO_COUNT), jnp.float32) ** block_levels(arg_keys[2], (3, LENGTHWISE_ALL, SECTORS_ALL, DEPTHWISE_COUNT, LOBATTO_COUNT * LOBATTO_COUNT * LOBATTO_COUNT), ((1, 8), (2, 16)), -0.2, 0.2)), 0.002, 0.02)
    inertia_over_timestep = jnp.clip(jnp.exp(math.log(1.0) - 2.3025851 * jax.random.uniform(arg_keys[3], (LENGTHWISE_ALL, SECTORS_ALL, DEPTHWISE_COUNT, LOBATTO_COUNT * LOBATTO_COUNT * LOBATTO_COUNT), jnp.float32) ** block_levels(arg_keys[3], (LENGTHWISE_ALL, SECTORS_ALL, DEPTHWISE_COUNT, LOBATTO_COUNT * LOBATTO_COUNT * LOBATTO_COUNT), ((0, 8), (1, 16)), -0.2, 0.2)), 0.1, 1.0)
    tracer_interval_index = place_ends(jax.random.randint(arg_keys[4], (3, PARTS_SIZE), 0, LOBATTO_COUNT - 1), jax.random.fold_in(arg_keys[4], 1), 0, (LOBATTO_COUNT - 1) - 1).astype(jnp.int32)
    tracer_interval_offset = jnp.clip(1.0 * jax.random.uniform(arg_keys[5], (3, PARTS_SIZE), jnp.float32) ** block_levels(arg_keys[5], (3, PARTS_SIZE), ((1, 128),), -0.2, 0.2), 0.0, 1.0)
    tracer_holding_chip_keys = jax.random.split(jax.random.fold_in(arg_keys[6], 1), PARTS_SIZE // P_DEV)
    tracer_holding_chip_turns = jax.random.permutation(jax.random.fold_in(arg_keys[6], 3), PARTS_SIZE // P_DEV)
    tracer_holding_chip = jax.vmap(lambda own, number: shared_out(jax.random.fold_in(arg_keys[6], 2), own, number, P_DEV, DEVICES, 1, CAP, 2))(tracer_holding_chip_keys, tracer_holding_chip_turns).reshape((PARTS_SIZE, 1))
    tracer_containing_piece = place_ends(jax.random.randint(arg_keys[7], (PARTS_SIZE,), 0, PIECES_ON_CHIP), jax.random.fold_in(arg_keys[7], 1), 0, PIECES_ON_CHIP - 1).astype(jnp.int32)
    chemical_shares = jnp.clip(0.2 + 0.8 * jax.random.uniform(arg_keys[8], (6, PARTS_SIZE), jnp.float32) ** block_levels(arg_keys[8], (6, PARTS_SIZE), ((1, 128),), -0.2, 0.2), 0.2, 1.0)
    frequency_scale = jnp.clip(jnp.exp(jax.random.uniform(arg_keys[9], (6,), jnp.float32, math.log(0.5), math.log(2.0))), 0.5, 2.0)
    energy_barrier = jnp.clip(jax.random.uniform(arg_keys[10], (6,), jnp.float32, 0.5, 2.0), 0.5, 2.0)
    return dict(flow_vector=flow_vector, thermal_state=thermal_state, stiffness_weights=stiffness_weights, inertia_over_timestep=inertia_over_timestep, tracer_interval_index=tracer_interval_index, tracer_interval_offset=tracer_interval_offset, tracer_holding_chip=tracer_holding_chip, tracer_containing_piece=tracer_containing_piece, chemical_shares=chemical_shares, frequency_scale=frequency_scale, energy_barrier=energy_barrier)


NODE_LIST = (-1.0, -0.8717401485096066, -0.5917001814331423, -0.2092992179024789, 0.2092992179024789, 0.5917001814331423, 0.8717401485096066, 1.0)
STEP_DT = 0.25


def bary_weights():
    nodes = np.array(NODE_LIST)
    weights = np.zeros(8)
    for idx_one in range(8):
        weights[idx_one] = 1.0 / np.prod([nodes[idx_one] - nodes[m] for m in range(8) if m != idx_one])
    return nodes, weights


def deriv_table():
    nodes, weights = bary_weights()
    lookup_matrix = np.zeros((8, 8))
    for row in range(8):
        for col in range(8):
            if row != col:
                lookup_matrix[row, col] = (weights[col] / weights[row]) / (nodes[row] - nodes[col])
        lookup_matrix[row, row] = -np.sum(lookup_matrix[row])
    return lookup_matrix


def lagrange(coord):
    nodes, weights = bary_weights()
    diffs = coord[:, None] - jnp.asarray(nodes, jnp.float32)[None, :]
    eye_mask = jnp.asarray(np.eye(8, dtype=bool))
    stacked = jnp.where(eye_mask[None, :, :], jnp.float32(1.0), diffs[:, None, :])
    return jnp.prod(stacked, axis=2) * jnp.asarray(weights, jnp.float32)[None, :]


def node_at(cells):
    nodes = jnp.asarray(np.array(NODE_LIST), jnp.float32)
    match = (cells[..., None] == jnp.arange(8, dtype=jnp.int32)).astype(jnp.float32)
    return jnp.sum(match * nodes, axis=-1)


def interp_rows(lookup_matrix, coords, index):
    hp = lax.Precision.HIGHEST
    rows = lookup_matrix[index].reshape(index.shape[0], 4, 8, 8, 8).astype(jnp.float32)
    first_w = lagrange(coords[0])
    second_w = lagrange(coords[1])
    third_w = lagrange(coords[2])
    segment_one = jnp.einsum('mfijk,mk->mfij', rows, third_w, precision=hp)
    segment_two = jnp.einsum('mfij,mj->mfi', segment_one, second_w, precision=hp)
    segment_three = jnp.einsum('mfi,mi->mf', segment_two, first_w, precision=hp)
    return segment_three.T


def helm_apply(field, geom, coef, dmat):
    hp = lax.Precision.HIGHEST
    d_one = jnp.einsum('pi,...ijk->...pjk', dmat, field, precision=hp)
    total = jnp.einsum('pi,...pjk->...ijk', dmat, geom[0] * d_one, precision=hp)
    d_two = jnp.einsum('pj,...ijk->...ipk', dmat, field, precision=hp)
    total = total + jnp.einsum('pj,...ipk->...ijk', dmat, geom[1] * d_two, precision=hp)
    d_three = jnp.einsum('pk,...ijk->...ijp', dmat, field, precision=hp)
    total = total + jnp.einsum('pk,...ijp->...ijk', dmat, geom[2] * d_three, precision=hp)
    return total + coef * field


def face_sum(field, edim, pdim, before, after):
    count = field.shape[edim]
    first = lax.index_in_dim(field, 0, pdim, keepdims=False)
    last = lax.index_in_dim(field, 7, pdim, keepdims=False)
    prev_last = jnp.concatenate([before, lax.slice_in_dim(last, 0, count - 1, axis=edim)], edim)
    next_first = jnp.concatenate([lax.slice_in_dim(first, 1, count, axis=edim), after], edim)
    new_first = first + prev_last
    new_last = last + next_first
    middle = lax.slice_in_dim(field, 1, 7, axis=pdim)
    return jnp.concatenate([jnp.expand_dims(new_first, pdim), middle, jnp.expand_dims(new_last, pdim)], pdim)


def assemble(field):
    shape_axial = (3, 1) + field.shape[2:4] + (8, 8)
    zeros_axial = jnp.zeros(shape_axial, jnp.float32)
    field = face_sum(field, 1, 4, zeros_axial, zeros_axial)
    first = lax.index_in_dim(field, 0, 5, keepdims=False)
    last = lax.index_in_dim(field, 7, 5, keepdims=False)
    field = face_sum(field, 2, 5, last[:, :, -1:], first[:, :, :1])
    shape_radial = field.shape[0:3] + (1, 8, 8)
    zeros_radial = jnp.zeros(shape_radial, jnp.float32)
    return face_sum(field, 3, 6, zeros_radial, zeros_radial)


def reference(flow_vector, thermal_state, stiffness_weights, inertia_over_timestep, tracer_interval_index, tracer_interval_offset, tracer_holding_chip, tracer_containing_piece, chemical_shares, frequency_scale, energy_barrier):
    dmat = jnp.asarray(deriv_table(), jnp.float32)
    shape_seven = (3, LENGTHWISE_ALL, SECTORS_ALL, DEPTHWISE_COUNT, 8, 8, 8)
    field = flow_vector.astype(jnp.float32).reshape(shape_seven)
    geom = stiffness_weights.reshape(shape_seven)
    coef = inertia_over_timestep.reshape(LENGTHWISE_ALL, SECTORS_ALL, DEPTHWISE_COUNT, 8, 8, 8)
    first_pass = assemble(helm_apply(field, geom, coef, dmat))
    second_pass = assemble(helm_apply(first_pass, geom, coef, dmat))
    velocity_out = second_pass.reshape(flow_vector.shape)

    flow_partitioned = flow_vector.reshape(3, N_AX, LENGTHWISE_CHIP, N_XS, SECTORS_CHIP, DEPTHWISE_COUNT, 512).transpose(1, 3, 2, 4, 5, 0, 6)
    flow_partitioned = flow_partitioned.reshape(DEVICES * PIECES_ON_CHIP, 3, 512)
    thermal_partitioned = thermal_state.reshape(N_AX, LENGTHWISE_CHIP, N_XS, SECTORS_CHIP, DEPTHWISE_COUNT, 512).transpose(0, 2, 1, 3, 4, 5)
    thermal_partitioned = thermal_partitioned.reshape(DEVICES * PIECES_ON_CHIP, 1, 512)
    lookup_matrix = jnp.concatenate([flow_partitioned, thermal_partitioned], 1).reshape(DEVICES * PIECES_ON_CHIP, 2048)

    low = node_at(tracer_interval_index)
    high = node_at(tracer_interval_index + 1)
    coords = low + tracer_interval_offset * (high - low)
    global_index = (tracer_holding_chip[:, 0] * PIECES_ON_CHIP + tracer_containing_piece).astype(jnp.int32)
    coord_blocks = coords.reshape(3, DEVICES, P_DEV).transpose(1, 0, 2)
    index_blocks = global_index.reshape(DEVICES, P_DEV)

    def one_block(pair):
        return interp_rows(lookup_matrix, pair[0], pair[1])

    probe = lax.map(one_block, (coord_blocks, index_blocks))
    probe = probe.transpose(1, 0, 2).reshape(4, PARTS_SIZE)
    coords_new = coords + STEP_DT * probe[0:3]
    rates = frequency_scale[:, None] * jnp.exp(energy_barrier[:, None] * jnp.tanh(probe[3][None, :] - 1.0))
    flux = rates * chemical_shares
    species_new = chemical_shares + STEP_DT * (jnp.roll(flux, 1, axis=0) - flux)
    return velocity_out, coords_new, species_new
```

```python
import functools

import jax
import jax.numpy as jnp
import numpy as np
from jax import lax
from jax.experimental import pallas as pl
from jax.experimental.pallas import tpu as pltpu
from jax.sharding import PartitionSpec as P

NODE_LIST = (
    -1.0,
    -0.8717401485096066,
    -0.5917001814331423,
    -0.2092992179024789,
    0.2092992179024789,
    0.5917001814331423,
    0.8717401485096066,
    1.0,
)
STEP_DT = 0.25
F32 = jnp.float32
BF16 = jnp.bfloat16
CHUNK = 256


def bary_weights():
    nodes = np.array(NODE_LIST)
    weights = np.zeros(8)
    for a in range(8):
        weights[a] = 1.0 / np.prod([nodes[a] - nodes[m] for m in range(8) if m != a])
    return nodes, weights


def deriv_table():
    nodes, weights = bary_weights()
    table = np.zeros((8, 8))
    for row in range(8):
        for col in range(8):
            if row != col:
                table[row, col] = weights[col] / weights[row] / (nodes[row] - nodes[col])
        table[row, row] = -np.sum(table[row])
    return table


DM = np.asarray(deriv_table(), np.float32).astype(np.float64)


def roll_tables():
    out = np.zeros((16, 8, 128), np.float32)
    for half, table in enumerate((DM, DM.T)):
        for s in range(8):
            for p in range(8):
                out[half * 8 + s, p, :] = table[p, (p - s) % 8]
    return out


def apply_table(table, u):
    even = [u[i] + u[7 - i] for i in range(4)]
    odd = [u[i] - u[7 - i] for i in range(4)]
    out = [None] * 8
    for p in range(4):
        a = b = None
        for i in range(4):
            ca = float((table[p, i] + table[p, 7 - i]) / 2)
            cb = float((table[p, i] - table[p, 7 - i]) / 2)
            ta, tb = even[i] * ca, odd[i] * cb
            a = ta if a is None else a + ta
            b = tb if b is None else b + tb
        out[p], out[7 - p] = a + b, b - a
    return out


def apply_rolls(tables, x):
    y = x * tables[0]
    for s in range(1, 8):
        y = y + pltpu.roll(x, s, 0) * tables[s]
    return y


def pick_node(cell, shift):
    out = jnp.full(cell.shape, NODE_LIST[shift], F32)
    for c in range(1, 7):
        out = jnp.where(cell == c, F32(NODE_LIST[c + shift]), out)
    return out


def split(x):
    high = x.astype(BF16).astype(F32)
    return high, x - high


def dispatch(idx_ref, off_ref, own_ref, piece_ref, coords_ref, rank_ref, pay_ref):
    total = idx_ref.shape[1]
    cell = idx_ref[...]
    low, high = pick_node(cell, 0), pick_node(cell, 1)
    coords_ref[...] = low + off_ref[...] * (high - low)
    rows = lax.broadcasted_iota(jnp.int32, (CHUNK, 2 * CHUNK), 0)
    cols = lax.broadcasted_iota(jnp.int32, (CHUNK, 2 * CHUNK), 1)
    before = jnp.where((rows < cols) | (cols >= CHUNK), 1.0, 0.0).astype(BF16)
    lane_id = lax.broadcasted_iota(jnp.int32, (128, CHUNK), 0)
    base = jnp.zeros((128, CHUNK), F32)
    for c in range(total // CHUNK):
        part = pl.ds(c * CHUNK, CHUNK)
        hot = jnp.where(own_ref[:, part] == lane_id, 1.0, 0.0)
        count = jnp.dot(hot.astype(BF16), before, preferred_element_type=F32)
        rank = jnp.sum(hot * (count[:, :CHUNK] + base), axis=0, keepdims=True)
        rank_ref[:, part] = rank.astype(jnp.int32)
        base = base + count[:, CHUNK:]
    pay_ref[...] = jnp.zeros_like(pay_ref)
    dims = (((1,), (1,)), ((), ()))
    for c in range(total // CHUNK):
        part = pl.ds(c * CHUNK, CHUNK)
        hot = jnp.where(own_ref[:, part] == lane_id, 1.0, 0.0).astype(BF16)
        mask = rank_ref[:, part] == lane_id
        tops, lows = [], []
        for d in range(3):
            high, rest = split(coords_ref[pl.ds(d, 1), part])
            tops.append(jnp.where(mask, high, 0.0).astype(BF16))
            lows.append(jnp.where(mask, rest, 0.0).astype(BF16))
        tops.append(jnp.where(mask, piece_ref[:, part].astype(F32), 0.0).astype(BF16))
        one = lax.dot_general(hot, jnp.concatenate(tops, 0), dims, preferred_element_type=F32)
        two = lax.dot_general(hot, jnp.concatenate(lows, 0), dims, preferred_element_type=F32)
        pay_ref[:, :384] += one[:, :384] + two
        pay_ref[:, 384:] += one[:, 384:]


def interpolate(got_ref, table_ref, back_ref, lag_ref, rows_ref):
    nodes, weights = bary_weights()
    ident = lax.broadcasted_iota(jnp.int32, (256, 256), 0)

    def block(b, carry):
        base = pl.multiple_of(b * 8, 8)
        for d in range(3):
            x = got_ref[pl.ds(base, 8), d * 128 : (d + 1) * 128]
            diff = [x - F32(n) for n in nodes]
            ahead, behind = [None] * 8, [None] * 8
            ahead[1], behind[6] = diff[0], diff[7]
            for i in range(2, 8):
                ahead[i] = ahead[i - 1] * diff[i - 1]
                behind[7 - i] = behind[8 - i] * diff[8 - i]
            for i in range(8):
                prod = behind[0] if i == 0 else ahead[7] if i == 7 else ahead[i] * behind[i]
                lag_ref[pl.ds(d * 64 + i * 8, 8), :] = prod * F32(weights[i])
        elem = got_ref[pl.ds(base, 8), 384:512].astype(jnp.int32)
        for pair in range(4):
            s0, s1 = 2 * pair, 2 * pair + 1
            ids = jnp.concatenate([elem[s0 : s0 + 1], elem[s1 : s1 + 1]], 1)
            hot = jnp.where(ident == ids, 1.0, 0.0).astype(BF16)

            def weight(d, i):
                row = d * 64 + i * 8
                return jnp.concatenate(
                    [lag_ref[pl.ds(row + s0, 1), :], lag_ref[pl.ds(row + s1, 1), :]], 1
                )

            third = jnp.concatenate(
                [lag_ref[pl.ds(128 + s0, 8, stride=8), :], lag_ref[pl.ds(128 + s1, 8, stride=8), :]], 1
            )
            for f in range(4):
                rows = jnp.dot(
                    table_ref[pl.ds(f * 512, 512), :], hot, preferred_element_type=F32
                )
                one = None
                for i in range(8):
                    term = rows[i * 64 : (i + 1) * 64] * weight(0, i)
                    one = term if one is None else one + term
                two = None
                for j in range(8):
                    term = one[j * 8 : (j + 1) * 8] * weight(1, j)
                    two = term if two is None else two + term
                value = jnp.sum(two * third, axis=0, keepdims=True)
                rows_ref[s0 : s0 + 1, f * 128 : (f + 1) * 128] = value[:, :128]
                rows_ref[s1 : s1 + 1, f * 128 : (f + 1) * 128] = value[:, 128:]
        back_ref[pl.ds(base, 8), :] = rows_ref[...]
        return carry

    lax.fori_loop(0, got_ref.shape[0] // 8, block, 0)


def combine(ret_ref, own_ref, rank_ref, coords_ref, share_ref, freq_ref, barrier_ref, cnew_ref, snew_ref, halves_ref):
    total = own_ref.shape[1]
    for f in range(4):
        turned = jnp.transpose(ret_ref[:, f * 128 : (f + 1) * 128])
        high, rest = split(turned)
        halves_ref[pl.ds(f * 128, 128), 0:128] = high.astype(BF16)
        halves_ref[pl.ds(f * 128, 128), 128:256] = rest.astype(BF16)
    lane_id = lax.broadcasted_iota(jnp.int32, (128, CHUNK), 0)
    freq, barrier = freq_ref[...], barrier_ref[...]
    for c in range(total // CHUNK):
        part = pl.ds(c * CHUNK, CHUNK)
        hot = jnp.where(own_ref[:, part] == lane_id, 1.0, 0.0).astype(BF16)
        found = jnp.dot(
            halves_ref[...], jnp.concatenate([hot, hot], 0), preferred_element_type=F32
        )
        mask = rank_ref[:, part] == lane_id
        probe = [
            jnp.sum(jnp.where(mask, found[f * 128 : (f + 1) * 128], 0.0), axis=0, keepdims=True)
            for f in range(4)
        ]
        for d in range(3):
            cnew_ref[pl.ds(d, 1), part] = coords_ref[pl.ds(d, 1), part] + STEP_DT * probe[d]
        rates = freq * jnp.exp(barrier * jnp.tanh(probe[3] - 1.0))
        shares = share_ref[:, part]
        flux = rates * shares
        moved = jnp.concatenate([flux[5:6], flux[0:5]], 0)
        snew_ref[:, part] = shares + STEP_DT * (moved - flux)


def turn_in(flow_ref, heat_ref, stiff_ref, inert_ref, x_ref, table_ref, g_ref, c_ref):
    def three(d, carry):
        for a in range(2):
            lanes = pl.ds(a * 128, 128)
            turned = jnp.transpose(flow_ref[d, lanes, :].astype(F32))
            x_ref[d, :, lanes] = turned
            table_ref[pl.ds(pl.multiple_of(d * 512, 512), 512), lanes] = turned.astype(BF16)
            g_ref[d, :, lanes] = jnp.transpose(stiff_ref[d, lanes, :])
        return carry

    lax.fori_loop(0, 3, three, 0)
    for a in range(2):
        lanes = pl.ds(a * 128, 128)
        table_ref[pl.ds(1536, 512), lanes] = jnp.transpose(heat_ref[lanes, :].astype(F32)).astype(BF16)
        c_ref[:, lanes] = jnp.transpose(inert_ref[lanes, :])


def helm(x_ref, g_ref, c_ref, t_ref, h_ref):
    def part(n, carry):
        f, a = n // 2, n % 2
        lanes = pl.ds(pl.multiple_of(a * 128, 128), 128)
        fore = [t_ref[s] for s in range(8)]
        aft = [t_ref[8 + s] for s in range(8)]
        for i in range(8):
            at = [pl.ds(i * 64 + j * 8, 8) for j in range(8)]
            x = [x_ref[f, at[j], lanes] for j in range(8)]
            dj = apply_table(DM, x)
            dj = [g_ref[1, at[j], lanes] * dj[j] for j in range(8)]
            dj = apply_table(DM.T, dj)
            for j in range(8):
                dk = g_ref[2, at[j], lanes] * apply_rolls(fore, x[j])
                h_ref[f, at[j], lanes] = dj[j] + c_ref[at[j], lanes] * x[j] + apply_rolls(aft, dk)
        for j in range(8):
            at = [pl.ds(i * 64 + j * 8, 8) for i in range(8)]
            di = apply_table(DM, [x_ref[f, at[i], lanes] for i in range(8)])
            di = [g_ref[0, at[i], lanes] * di[i] for i in range(8)]
            di = apply_table(DM.T, di)
            for i in range(8):
                h_ref[f, at[i], lanes] += di[i]
        return carry

    lax.fori_loop(0, 6, part, 0)


def faces(h_ref, low_ref, high_ref, left_ref, right_ref):
    for f in range(3):
        low_ref[f] = h_ref[f, 0:64, 0:128]
        high_ref[f] = h_ref[f, 448:512, 128:256]
        both = h_ref[f, 448:512, 0:128] + h_ref[f, 0:64, 128:256]
        h_ref[f, 448:512, 0:128] = both
        h_ref[f, 0:64, 128:256] = both
    lane = lax.broadcasted_iota(jnp.int32, (8, 128), 1) // 32

    def pack(n, carry):
        f, a = n // 2, n % 2
        lanes = pl.ds(pl.multiple_of(a * 128, 128), 128)
        for half in range(2):
            one = two = None
            for q in range(4):
                row = (half * 4 + q) * 64
                first = h_ref[f, pl.ds(row, 8), lanes]
                last = h_ref[f, pl.ds(row + 56, 8), lanes]
                if q:
                    first = pltpu.roll(first, 32 * q, 1)
                if q < 3:
                    last = pltpu.roll(last, 32 * q + 32, 1)
                one = first if one is None else jnp.where(lane == q, first, one)
                two = last if two is None else jnp.where(lane == q, last, two)
            left_ref[f, a, half] = one
            right_ref[f, a, half] = two
        return carry

    lax.fori_loop(0, 6, pack, 0)


def assemble(h_ref, x_ref, low_ref, high_ref, left_ref, right_ref, corner):
    lane = lax.broadcasted_iota(jnp.int32, (8, 128), 1)
    sub = lax.broadcasted_iota(jnp.int32, (8, 128), 0)
    quarter, radial = lane // 32, lane % 32
    at_first = (sub == 0) & (radial != 0)
    at_last = (sub == 7) & (radial != 31)

    def near(f, carry):
        h_ref[f, 0:64, 0:128] += low_ref[f]
        h_ref[f, 448:512, 128:256] += high_ref[f]
        left_ref[f, 0, 0] += jnp.where(quarter == 0, pltpu.roll(corner(0)[f], 32, 1), 0.0)
        left_ref[f, 1, 1] += jnp.where(quarter == 3, pltpu.roll(corner(1)[f], 96, 1), 0.0)
        right_ref[f, 0, 0] += jnp.where(quarter == 0, pltpu.roll(corner(2)[f], 32, 1), 0.0)
        right_ref[f, 1, 1] += jnp.where(quarter == 3, pltpu.roll(corner(3)[f], 96, 1), 0.0)
        return carry

    lax.fori_loop(0, 3, near, 0)

    def radially(x):
        up = pltpu.roll(pltpu.roll(x, 1, 1), 1, 0)
        down = pltpu.roll(pltpu.roll(x, 127, 1), 7, 0)
        return x + jnp.where(at_first, up, 0.0) + jnp.where(at_last, down, 0.0)

    def part(n, carry):
        f, a = n // 2, n % 2
        lanes = pl.ds(pl.multiple_of(a * 128, 128), 128)
        for i in range(8):
            half, q = i // 4, i % 4
            first = h_ref[f, pl.ds(i * 64, 8), lanes]
            last = h_ref[f, pl.ds(i * 64 + 56, 8), lanes]
            before, after = left_ref[f, a, half], right_ref[f, a, half]
            if q:
                before = pltpu.roll(before, 128 - 32 * q, 1)
            if q < 3:
                after = pltpu.roll(after, 96 - 32 * q, 1)
            before = jnp.where(quarter == 0, before, pltpu.roll(last, 32, 1))
            after = jnp.where(quarter == 3, after, pltpu.roll(first, 96, 1))
            x_ref[f, pl.ds(i * 64, 8), lanes] = radially(first + before)
            x_ref[f, pl.ds(i * 64 + 56, 8), lanes] = radially(last + after)
            for j in range(1, 7):
                row = pl.ds(i * 64 + j * 8, 8)
                x_ref[f, row, lanes] = radially(h_ref[f, row, lanes])
        return carry

    lax.fori_loop(0, 6, part, 0)


def turn_out(x_ref, out_ref):
    def three(d, carry):
        for a in range(2):
            lanes = pl.ds(a * 128, 128)
            out_ref[d, lanes, :] = jnp.transpose(x_ref[d, :, lanes])
        return carry

    lax.fori_loop(0, 3, three, 0)


def call(body, outs, scratch, *args):
    vmem = pl.BlockSpec(memory_space=pltpu.VMEM)
    return pl.pallas_call(
        body,
        out_shape=[jax.ShapeDtypeStruct(shape, dtype) for shape, dtype in outs],
        in_specs=[vmem] * len(args),
        out_specs=[vmem] * len(outs),
        scratch_shapes=[pltpu.VMEM(shape, dtype) for shape, dtype in scratch],
        compiler_params=pltpu.CompilerParams(vmem_limit_bytes=48 * 1024 * 1024),
    )(*args)


FIELD = ((3, 512, 256), F32)
FACE = ((3, 64, 128), F32)
SIDE = ((3, 2, 2, 8, 128), F32)
FACES = [FACE, FACE, SIDE, SIDE]


def first_body(flow, heat, stiff, inert, tables, h, table, g, c, low, high, left, right, x):
    turn_in(flow, heat, stiff, inert, x, table, g, c)
    helm(x, g, c, tables, h)
    faces(h, low, high, left, right)


def second_body(h1, g, c, tables, low1, high1, left1, right1, corners, h, low, high, left, right, x, work, l1, r1):
    work[...] = h1[...]
    l1[...] = left1[...]
    r1[...] = right1[...]
    assemble(work, x, low1, high1, l1, r1, lambda n: corners.at[n])
    helm(x, g, c, tables, h)
    faces(h, low, high, left, right)


def last_body(h1, low1, high1, left1, right1, corners, out, x, work, l1, r1):
    work[...] = h1[...]
    l1[...] = left1[...]
    r1[...] = right1[...]
    assemble(work, x, low1, high1, l1, r1, lambda n: corners.at[n])
    turn_out(x, out)


def exchange(low, high, left, right):
    n_ax, n_xs = lax.axis_size("ax"), lax.axis_size("xs")

    def shift(value, da, dx):
        if da == 0:
            pairs = [(i, (i + dx) % n_xs) for i in range(n_xs)]
            return lax.ppermute(value, "xs", pairs)
        if dx == 0:
            pairs = [(i, i + da) for i in range(n_ax) if 0 <= i + da < n_ax]
            return lax.ppermute(value, "ax", pairs)
        pairs = [
            (i * n_xs + j, (i + da) * n_xs + (j + dx) % n_xs)
            for i in range(n_ax)
            for j in range(n_xs)
            if 0 <= i + da < n_ax
        ]
        return lax.ppermute(value, ("ax", "xs"), pairs)

    corners = jnp.stack(
        [
            shift(right[:, 1, 1], 1, 1),
            shift(right[:, 0, 0], -1, 1),
            shift(left[:, 1, 1], 1, -1),
            shift(left[:, 0, 0], -1, -1),
        ]
    )
    return shift(high, 1, 0), shift(low, -1, 0), shift(right, 0, 1), shift(left, 0, -1), corners


def local(flow, heat, stiff, inert, index, offset, owner, piece, shares, freq, barrier):
    particles = piece.shape[0]
    flow3 = flow.reshape(3, 256, 512)
    heat2 = heat.reshape(256, 512)
    stiff3 = stiff.reshape(3, 256, 512)
    inert2 = inert.reshape(256, 512)
    owner = owner.reshape(1, particles)
    piece = piece.reshape(1, particles)
    tables = jnp.asarray(roll_tables())
    coords, rank, payload = call(
        dispatch,
        [((3, particles), F32), ((1, particles), jnp.int32), ((128, 512), F32)],
        [],
        index,
        offset,
        owner,
        piece,
    )
    received = lax.all_to_all(payload, ("ax", "xs"), split_axis=0, concat_axis=0, tiled=True)
    h, table, g, c, *rims = call(
        first_body,
        [FIELD, ((2048, 256), BF16), FIELD, ((512, 256), F32)] + FACES,
        [FIELD],
        flow3,
        heat2,
        stiff3,
        inert2,
        tables,
    )
    rims = exchange(*rims)
    (values,) = call(interpolate, [((128, 512), F32)], [((192, 128), F32), ((8, 512), F32)], received, table)
    returned = lax.all_to_all(values, ("ax", "xs"), split_axis=0, concat_axis=0, tiled=True)
    h, *rims = call(
        second_body, [FIELD] + FACES, [FIELD, FIELD, SIDE, SIDE], h, g, c, tables, *rims
    )
    rims = exchange(*rims)
    cnew, snew = call(
        combine,
        [((3, particles), F32), ((6, particles), F32)],
        [((512, 256), BF16)],
        returned,
        owner,
        rank,
        coords,
        shares,
        freq.reshape(6, 1),
        barrier.reshape(6, 1),
    )
    (out,) = call(last_body, [((3, 256, 512), F32)], [FIELD, FIELD, SIDE, SIDE], h, *rims)
    return out.reshape(flow.shape), cnew, snew


def solution(mesh):
    placed = (
        P(None, "ax", "xs", None, None),
        P("ax", "xs", None, None),
        P(None, "ax", "xs", None, None),
        P("ax", "xs", None, None),
        P(None, ("ax", "xs")),
        P(None, ("ax", "xs")),
        P(("ax", "xs"), None),
        P(("ax", "xs")),
        P(None, ("ax", "xs")),
        P(),
        P(),
    )
    return jax.shard_map(
        local,
        mesh=mesh,
        in_specs=placed,
        out_specs=(P(None, "ax", "xs", None, None), P(None, ("ax", "xs")), P(None, ("ax", "xs"))),
        check_vma=False,
    )
```

```python
import functools

import jax
import jax.numpy as jnp
import numpy as np
from jax import lax
from jax.experimental import pallas as pl
from jax.experimental.pallas import tpu as pltpu
from jax.sharding import PartitionSpec as P

NODE_LIST = (
    -1.0,
    -0.8717401485096066,
    -0.5917001814331423,
    -0.2092992179024789,
    0.2092992179024789,
    0.5917001814331423,
    0.8717401485096066,
    1.0,
)
STEP_DT = 0.25
F32 = jnp.float32
BF16 = jnp.bfloat16
CHUNK = 256


def bary_weights():
    nodes = np.array(NODE_LIST)
    weights = np.zeros(8)
    for a in range(8):
        weights[a] = 1.0 / np.prod([nodes[a] - nodes[m] for m in range(8) if m != a])
    return nodes, weights


def deriv_table():
    nodes, weights = bary_weights()
    table = np.zeros((8, 8))
    for row in range(8):
        for col in range(8):
            if row != col:
                table[row, col] = weights[col] / weights[row] / (nodes[row] - nodes[col])
        table[row, row] = -np.sum(table[row])
    return table


DM = np.asarray(deriv_table(), np.float32).astype(np.float64)


def fill_tables(t_ref):
    sub = lax.broadcasted_iota(jnp.int32, (8, 128), 0)
    for half, table in enumerate((DM, DM.T)):
        for s in range(8):
            out = jnp.full((8, 128), table[0, (0 - s) % 8], F32)
            for p in range(1, 8):
                out = jnp.where(sub == p, F32(table[p, (p - s) % 8]), out)
            t_ref[half * 8 + s] = out


def apply_table(table, u):
    even = [u[i] + u[7 - i] for i in range(4)]
    odd = [u[i] - u[7 - i] for i in range(4)]
    out = [None] * 8
    for p in range(4):
        a = b = None
        for i in range(4):
            ca = float((table[p, i] + table[p, 7 - i]) / 2)
            cb = float((table[p, i] - table[p, 7 - i]) / 2)
            ta, tb = even[i] * ca, odd[i] * cb
            a = ta if a is None else a + ta
            b = tb if b is None else b + tb
        out[p], out[7 - p] = a + b, b - a
    return out


def apply_rolls(tables, x):
    y = x * tables[0]
    for s in range(1, 8):
        y = y + pltpu.roll(x, s, 0) * tables[s]
    return y


def pick_node(cell, shift):
    out = jnp.full(cell.shape, NODE_LIST[shift], F32)
    for c in range(1, 7):
        out = jnp.where(cell == c, F32(NODE_LIST[c + shift]), out)
    return out


def split(x):
    high = x.astype(BF16).astype(F32)
    return high, x - high


def dispatch(idx_ref, off_ref, own_ref, piece_ref, coords_ref, rank_ref, pay_ref):
    total = idx_ref.shape[1]
    cell = idx_ref[...]
    low, high = pick_node(cell, 0), pick_node(cell, 1)
    coords_ref[...] = low + off_ref[...] * (high - low)
    rows = lax.broadcasted_iota(jnp.int32, (CHUNK, 2 * CHUNK), 0)
    cols = lax.broadcasted_iota(jnp.int32, (CHUNK, 2 * CHUNK), 1)
    before = jnp.where((rows < cols) | (cols >= CHUNK), 1.0, 0.0).astype(BF16)
    lane_id = lax.broadcasted_iota(jnp.int32, (128, CHUNK), 0)
    base = jnp.zeros((128, CHUNK), F32)
    for c in range(total // CHUNK):
        part = pl.ds(c * CHUNK, CHUNK)
        hot = jnp.where(own_ref[:, part] == lane_id, 1.0, 0.0)
        count = jnp.dot(hot.astype(BF16), before, preferred_element_type=F32)
        rank = jnp.sum(hot * (count[:, :CHUNK] + base), axis=0, keepdims=True)
        rank_ref[:, part] = rank.astype(jnp.int32)
        base = base + count[:, CHUNK:]
    sums = [jnp.zeros((128, 128), F32)] * 4
    dims = (((1,), (1,)), ((), ()))
    for c in range(total // CHUNK):
        part = pl.ds(c * CHUNK, CHUNK)
        hot = jnp.where(own_ref[:, part] == lane_id, 1.0, 0.0).astype(BF16)
        mask = rank_ref[:, part] == lane_id
        tops, lows = [], []
        for d in range(3):
            high, rest = split(coords_ref[pl.ds(d, 1), part])
            tops.append(jnp.where(mask, high, 0.0).astype(BF16))
            lows.append(jnp.where(mask, rest, 0.0).astype(BF16))
        tops.append(jnp.where(mask, piece_ref[:, part].astype(F32), 0.0).astype(BF16))
        one = lax.dot_general(hot, jnp.concatenate(tops, 0), dims, preferred_element_type=F32)
        two = lax.dot_general(hot, jnp.concatenate(lows, 0), dims, preferred_element_type=F32)
        sums = [
            sums[v] + (one[:, v * 128 : (v + 1) * 128] + two[:, v * 128 : (v + 1) * 128] if v < 3 else one[:, 384:])
            for v in range(4)
        ]
    for v in range(4):
        pay_ref[:, v, :] = sums[v]


def interpolate(base, got_ref, table_ref, back_ref, lag_ref):
    nodes, weights = bary_weights()
    ident = lax.broadcasted_iota(jnp.int32, (256, 256), 0)
    for d in range(3):
        x = got_ref[pl.ds(base, 8), d, :]
        diff = [x - F32(n) for n in nodes]
        ahead, behind = [None] * 8, [None] * 8
        ahead[1], behind[6] = diff[0], diff[7]
        for i in range(2, 8):
            ahead[i] = ahead[i - 1] * diff[i - 1]
            behind[7 - i] = behind[8 - i] * diff[8 - i]
        for i in range(8):
            prod = behind[0] if i == 0 else ahead[7] if i == 7 else ahead[i] * behind[i]
            lag_ref[pl.ds(d * 64 + i * 8, 8), :] = prod * F32(weights[i])
    elem = got_ref[pl.ds(base, 8), 3, :].astype(jnp.int32)
    for pair in range(4):
        s0, s1 = 2 * pair, 2 * pair + 1
        ids = jnp.concatenate([elem[s0 : s0 + 1], elem[s1 : s1 + 1]], 1)
        hot = jnp.where(ident == ids, 1.0, 0.0).astype(BF16)

        def weight(d, i):
            row = d * 64 + i * 8
            return jnp.concatenate(
                [lag_ref[pl.ds(row + s0, 1), :], lag_ref[pl.ds(row + s1, 1), :]], 1
            )

        third = jnp.concatenate(
            [lag_ref[pl.ds(128 + s0, 8, stride=8), :], lag_ref[pl.ds(128 + s1, 8, stride=8), :]], 1
        )
        for f in range(4):
            rows = jnp.dot(table_ref[pl.ds(f * 512, 512), :], hot, preferred_element_type=F32)
            one = None
            for i in range(8):
                term = rows[i * 64 : (i + 1) * 64] * weight(0, i)
                one = term if one is None else one + term
            two = None
            for j in range(8):
                term = one[j * 8 : (j + 1) * 8] * weight(1, j)
                two = term if two is None else two + term
            value = jnp.sum(two * third, axis=0, keepdims=True)
            back_ref[base + s0, pl.ds(f, 1), :] = value[:, :128]
            back_ref[base + s1, pl.ds(f, 1), :] = value[:, 128:]


def gather_back(ret_ref, own_ref, rank_ref, probe_ref, halves_ref):
    total = own_ref.shape[1]
    for f in range(4):
        high, rest = split(jnp.transpose(ret_ref[:, f, :]))
        halves_ref[pl.ds(f * 128, 128), 0:128] = high.astype(BF16)
        halves_ref[pl.ds(f * 128, 128), 128:256] = rest.astype(BF16)
    lane_id = lax.broadcasted_iota(jnp.int32, (128, CHUNK), 0)
    for c in range(total // CHUNK):
        part = pl.ds(c * CHUNK, CHUNK)
        hot = jnp.where(own_ref[:, part] == lane_id, 1.0, 0.0).astype(BF16)
        found = jnp.dot(
            halves_ref[...], jnp.concatenate([hot, hot], 0), preferred_element_type=F32
        )
        mask = rank_ref[:, part] == lane_id
        for f in range(4):
            kept = jnp.where(mask, found[f * 128 : (f + 1) * 128], 0.0)
            probe_ref[pl.ds(f, 1), part] = jnp.sum(kept, axis=0, keepdims=True)


def kinetics(probe_ref, coords_ref, share_ref, freq_ref, barrier_ref, cnew_ref, snew_ref):
    cnew_ref[...] = coords_ref[...] + STEP_DT * probe_ref[0:3, :]
    rates = freq_ref[...] * jnp.exp(barrier_ref[...] * jnp.tanh(probe_ref[3:4, :] - 1.0))
    shares = share_ref[...]
    flux = rates * shares
    moved = jnp.concatenate([flux[5:6], flux[0:5]], 0)
    snew_ref[...] = shares + STEP_DT * (moved - flux)


def turn_in(flow_ref, heat_ref, stiff_ref, inert_ref, x_ref, table_ref, g_ref, c_ref):
    def three(d, carry):
        for a in range(2):
            lanes = pl.ds(a * 128, 128)
            turned = jnp.transpose(flow_ref[d, lanes, :].astype(F32))
            x_ref[d, :, lanes] = turned
            table_ref[pl.ds(pl.multiple_of(d * 512, 512), 512), lanes] = turned.astype(BF16)
            g_ref[d, :, lanes] = jnp.transpose(stiff_ref[d, lanes, :])
        return carry

    lax.fori_loop(0, 3, three, 0)
    for a in range(2):
        lanes = pl.ds(a * 128, 128)
        table_ref[pl.ds(1536, 512), lanes] = jnp.transpose(heat_ref[lanes, :].astype(F32)).astype(BF16)
        c_ref[:, lanes] = jnp.transpose(inert_ref[lanes, :])


def helm(x_ref, g_ref, c_ref, t_ref, h_ref):
    def part(n, carry):
        f, a = n // 2, n % 2
        lanes = pl.ds(pl.multiple_of(a * 128, 128), 128)
        fore = [t_ref[s] for s in range(8)]
        aft = [t_ref[8 + s] for s in range(8)]
        for i in range(8):
            at = [pl.ds(i * 64 + j * 8, 8) for j in range(8)]
            x = [x_ref[f, at[j], lanes] for j in range(8)]
            dj = apply_table(DM, x)
            dj = [g_ref[1, at[j], lanes] * dj[j] for j in range(8)]
            dj = apply_table(DM.T, dj)
            for j in range(8):
                dk = g_ref[2, at[j], lanes] * apply_rolls(fore, x[j])
                h_ref[f, at[j], lanes] = dj[j] + c_ref[at[j], lanes] * x[j] + apply_rolls(aft, dk)
        for j in range(8):
            at = [pl.ds(i * 64 + j * 8, 8) for i in range(8)]
            di = apply_table(DM, [x_ref[f, at[i], lanes] for i in range(8)])
            di = [g_ref[0, at[i], lanes] * di[i] for i in range(8)]
            di = apply_table(DM.T, di)
            for i in range(8):
                h_ref[f, at[i], lanes] += di[i]
        return carry

    lax.fori_loop(0, 6, part, 0)


def faces(h_ref, low_ref, high_ref, left_ref, right_ref):
    for f in range(3):
        low_ref[f] = h_ref[f, 0:64, 0:128]
        high_ref[f] = h_ref[f, 448:512, 128:256]
        both = h_ref[f, 448:512, 0:128] + h_ref[f, 0:64, 128:256]
        h_ref[f, 448:512, 0:128] = both
        h_ref[f, 0:64, 128:256] = both
    lane = lax.broadcasted_iota(jnp.int32, (8, 128), 1) // 32

    def pack(n, carry):
        f, a = n // 2, n % 2
        lanes = pl.ds(pl.multiple_of(a * 128, 128), 128)
        for half in range(2):
            one = two = None
            for q in range(4):
                row = (half * 4 + q) * 64
                first = h_ref[f, pl.ds(row, 8), lanes]
                last = h_ref[f, pl.ds(row + 56, 8), lanes]
                if q:
                    first = pltpu.roll(first, 32 * q, 1)
                if q < 3:
                    last = pltpu.roll(last, 32 * q + 32, 1)
                one = first if one is None else jnp.where(lane == q, first, one)
                two = last if two is None else jnp.where(lane == q, last, two)
            left_ref[f, a, half] = one
            right_ref[f, a, half] = two
        return carry

    lax.fori_loop(0, 6, pack, 0)


def assemble(h_ref, x_ref, low_ref, high_ref, left_ref, right_ref, corner_ref, lowest, highest):
    lane = lax.broadcasted_iota(jnp.int32, (8, 128), 1)
    sub = lax.broadcasted_iota(jnp.int32, (8, 128), 0)
    quarter, radial = lane // 32, lane % 32
    at_first = (sub == 0) & (radial != 0)
    at_last = (sub == 7) & (radial != 31)

    under = jnp.where(lowest, F32(0.0), F32(1.0))
    over = jnp.where(highest, F32(0.0), F32(1.0))

    def near(f, carry):
        def corner(n, q, turn, scale):
            return jnp.where(quarter == q, pltpu.roll(corner_ref[n, f], turn, 1) * scale, 0.0)

        h_ref[f, 0:64, 0:128] += low_ref[f] * under
        h_ref[f, 448:512, 128:256] += high_ref[f] * over
        left_ref[f, 0, 0] += corner(0, 0, 32, under)
        left_ref[f, 1, 1] += corner(1, 3, 96, over)
        right_ref[f, 0, 0] += corner(2, 0, 32, under)
        right_ref[f, 1, 1] += corner(3, 3, 96, over)
        return carry

    lax.fori_loop(0, 3, near, 0)

    def radially(x):
        up = pltpu.roll(pltpu.roll(x, 1, 1), 1, 0)
        down = pltpu.roll(pltpu.roll(x, 127, 1), 7, 0)
        return x + jnp.where(at_first, up, 0.0) + jnp.where(at_last, down, 0.0)

    def part(n, carry):
        f, a = n // 2, n % 2
        lanes = pl.ds(pl.multiple_of(a * 128, 128), 128)
        for i in range(8):
            half, q = i // 4, i % 4
            first = h_ref[f, pl.ds(i * 64, 8), lanes]
            last = h_ref[f, pl.ds(i * 64 + 56, 8), lanes]
            before, after = left_ref[f, a, half], right_ref[f, a, half]
            if q:
                before = pltpu.roll(before, 128 - 32 * q, 1)
            if q < 3:
                after = pltpu.roll(after, 96 - 32 * q, 1)
            before = jnp.where(quarter == 0, before, pltpu.roll(last, 32, 1))
            after = jnp.where(quarter == 3, after, pltpu.roll(first, 96, 1))
            x_ref[f, pl.ds(i * 64, 8), lanes] = radially(first + before)
            x_ref[f, pl.ds(i * 64 + 56, 8), lanes] = radially(last + after)
            for j in range(1, 7):
                row = pl.ds(i * 64 + j * 8, 8)
                x_ref[f, row, lanes] = radially(h_ref[f, row, lanes])
        return carry

    lax.fori_loop(0, 6, part, 0)


FIELD = ((3, 512, 256), F32)
FACE = ((3, 64, 128), F32)
SIDE = ((3, 2, 2, 8, 128), F32)
CORNER = ((4, 3, 8, 128), F32)
RIMS = [FACE, FACE, SIDE, SIDE]
SLOTS = ((128, 4, 128), F32)
MESH = pl.DeviceIdType.MESH
LIMIT = 56 * 1024 * 1024


def rim_copies(n_ax, n_xs, sent, landed, corners, send_sems, recv_sems):
    ax, xs = lax.axis_index("ax"), lax.axis_index("xs")
    low, high, left, right = sent
    plan = [
        (high, landed[0], 1, 0),
        (low, landed[1], -1, 0),
        (right, landed[2], 0, 1),
        (left, landed[3], 0, -1),
        (right.at[:, 1, 1], corners.at[0], 1, 1),
        (right.at[:, 0, 0], corners.at[1], -1, 1),
        (left.at[:, 1, 1], corners.at[2], 1, -1),
        (left.at[:, 0, 0], corners.at[3], -1, -1),
    ]
    return [
        pltpu.make_async_remote_copy(
            src_ref=src,
            dst_ref=dst,
            send_sem=send_sems.at[n],
            recv_sem=recv_sems.at[n],
            device_id=(lax.rem(ax + da + n_ax, n_ax), lax.rem(xs + dx + n_xs, n_xs)),
            device_id_type=MESH,
        )
        for n, (src, dst, da, dx) in enumerate(plan)
    ]


def main_body(n_ax, n_xs, *refs):
    (flow_h, heat_h, stiff_h, inert_h, idx_h, off_h, own_h, piece_h) = refs[:8]
    (h2, low4, high4, left4, right4, corners2, probe, coords) = refs[8:16]
    (flow, heat, stiff, inert, idx, off, own, piece) = refs[16:24]
    (rank, pay, got, back, ret, x, h, g, c, table, tables, lag, halves) = refs[24:37]
    (low1, high1, left1, right1, low2, high2, left2, right2, corners1) = refs[37:46]
    (low3, high3, left3, right3) = refs[46:50]
    (in_sems, out_send, out_recv, back_send, back_recv, rim_send, rim_recv) = refs[50:]
    devices = n_ax * n_xs
    ax, xs = lax.axis_index("ax"), lax.axis_index("xs")
    me = ax * n_xs + xs

    loads = [
        pltpu.make_async_copy(src, dst, in_sems.at[n])
        for n, (src, dst) in enumerate(
            zip(
                (idx_h, off_h, own_h, piece_h, flow_h, heat_h, stiff_h, inert_h),
                (idx, off, own, piece, flow, heat, stiff, inert),
            )
        )
    ]
    for load in loads:
        load.start()

    def where(n):
        return (lax.div(n, n_xs), lax.rem(n, n_xs))

    barrier = pltpu.get_barrier_semaphore()

    def greet(k, carry):
        pl.semaphore_signal(
            barrier, inc=1, device_id=where(lax.rem(me + k, devices)), device_id_type=MESH
        )
        return carry

    lax.fori_loop(1, devices, greet, 0)
    fill_tables(tables)
    for load in loads[:4]:
        load.wait()
    dispatch(idx, off, own, piece, coords, rank, pay)
    pl.semaphore_wait(barrier, devices - 1)

    group = lax.div(me, 8)
    own_copy = pltpu.make_async_copy(pay.at[me], got.at[me], out_recv.at[group])
    own_copy.start()

    def send(k, carry):
        to = lax.rem(me + k, devices)
        pltpu.make_async_remote_copy(
            src_ref=pay.at[to],
            dst_ref=got.at[me],
            send_sem=out_send,
            recv_sem=out_recv.at[group],
            device_id=where(to),
            device_id_type=MESH,
        ).start()
        return carry

    lax.fori_loop(1, devices, send, 0)

    for load in loads[4:]:
        load.wait()
    turn_in(flow, heat, stiff, inert, x, table, g, c)
    helm(x, g, c, tables, h)
    faces(h, low1, high1, left1, right1)
    first = rim_copies(
        n_ax, n_xs, (low1, high1, left1, right1), (low2, high2, left2, right2), corners1,
        rim_send.at[0], rim_recv.at[0],
    )
    for copy in first:
        copy.start()

    def block(n, carry):
        now = lax.rem(group + 2 * (devices // 8) - 1 - n, devices // 8)
        base = now * 8
        rows = got.at[pl.ds(base, 8)]
        pltpu.make_async_copy(rows, rows, out_recv.at[now]).wait()
        interpolate(base, got, table, back, lag)

        def give(s, inner):
            to = base + s

            @pl.when(to != me)
            def _():
                pltpu.make_async_remote_copy(
                    src_ref=back.at[to],
                    dst_ref=ret.at[me],
                    send_sem=back_send,
                    recv_sem=back_recv,
                    device_id=where(to),
                    device_id_type=MESH,
                ).start()

            @pl.when(to == me)
            def _():
                pltpu.make_async_copy(back.at[to], ret.at[me], back_recv).start()

            return inner

        lax.fori_loop(0, 8, give, 0)
        return carry

    lax.fori_loop(0, devices // 8, block, 0)

    for copy in first:
        copy.wait()
    assemble(h, x, low2, high2, left2, right2, corners1, ax == 0, ax == n_ax - 1)
    helm(x, g, c, tables, h2)
    faces(h2, low3, high3, left3, right3)
    second = rim_copies(
        n_ax, n_xs, (low3, high3, left3, right3), (low4, high4, left4, right4), corners2,
        rim_send.at[1], rim_recv.at[1],
    )
    for copy in second:
        copy.start()

    pltpu.make_async_copy(ret, ret, back_recv).wait()
    gather_back(ret, own, rank, probe, halves)

    others = pl.ds(0, devices - 1)
    pltpu.make_async_copy(pay.at[others], pay.at[others], out_send).wait()
    pltpu.make_async_copy(back.at[others], back.at[others], back_send).wait()
    for copy in second:
        copy.wait()


def last_body(h1, low1, high1, left1, right1, corners, probe, coords, shares, freq, barrier, out, cnew, snew, x, work, l1, r1, turned, sems):
    ax, n_ax = lax.axis_index("ax"), lax.axis_size("ax")
    kinetics(probe, coords, shares, freq, barrier, cnew, snew)
    work[...] = h1[...]
    l1[...] = left1[...]
    r1[...] = right1[...]
    assemble(work, x, low1, high1, l1, r1, corners, ax == 0, ax == n_ax - 1)
    copies = []
    for d in range(3):
        for a in range(2):
            lanes = pl.ds(a * 128, 128)
            turned[d, lanes, :] = jnp.transpose(x[d, :, lanes])
            copy = pltpu.make_async_copy(turned.at[d, lanes], out.at[d, lanes], sems.at[d * 2 + a])
            copy.start()
            copies.append(copy)
    for copy in copies:
        copy.wait()


def shapes(outs):
    return [jax.ShapeDtypeStruct(shape, dtype) for shape, dtype in outs]


def buffers(outs):
    return [pltpu.VMEM(shape, dtype) for shape, dtype in outs]


def local(flow, heat, stiff, inert, index, offset, owner, piece, shares, freq, barrier):
    particles = piece.shape[0]
    n_ax, n_xs = lax.axis_size("ax"), lax.axis_size("xs")
    devices = n_ax * n_xs
    vmem = pl.BlockSpec(memory_space=pltpu.VMEM)
    hbm = pl.BlockSpec(memory_space=pltpu.HBM)
    inputs = (
        flow.reshape(3, 256, 512),
        heat.reshape(256, 512),
        stiff.reshape(3, 256, 512),
        inert.reshape(256, 512),
        index,
        offset,
        owner.reshape(1, particles),
        piece.reshape(1, particles),
    )
    held = [(a.shape, a.dtype) for a in inputs]
    table = ((2048, 256), BF16)
    outs = [FIELD, *RIMS, CORNER, ((4, particles), F32), ((3, particles), F32)]
    passed = pl.pallas_call(
        functools.partial(main_body, n_ax, n_xs),
        out_shape=shapes(outs),
        in_specs=[hbm] * 8,
        out_specs=[vmem] * len(outs),
        scratch_shapes=buffers(held)
        + buffers([((1, particles), jnp.int32), SLOTS, SLOTS, SLOTS, SLOTS, FIELD, FIELD, FIELD])
        + buffers([((512, 256), F32), table, ((16, 8, 128), F32), ((192, 128), F32), ((512, 256), BF16)])
        + buffers([*RIMS, *RIMS, CORNER, *RIMS])
        + [
            pltpu.SemaphoreType.DMA((8,)),
            pltpu.SemaphoreType.DMA,
            pltpu.SemaphoreType.DMA((devices // 8,)),
            pltpu.SemaphoreType.DMA,
            pltpu.SemaphoreType.DMA,
            pltpu.SemaphoreType.DMA((2, 8)),
            pltpu.SemaphoreType.DMA((2, 8)),
        ],
        compiler_params=pltpu.CompilerParams(
            collective_id=0, has_side_effects=True, vmem_limit_bytes=LIMIT
        ),
    )(*inputs)
    outs = [((3, 256, 512), F32), ((3, particles), F32), ((6, particles), F32)]
    out, cnew, snew = pl.pallas_call(
        last_body,
        out_shape=shapes(outs),
        in_specs=[vmem] * 11,
        out_specs=[hbm, vmem, vmem],
        scratch_shapes=buffers([FIELD, FIELD, SIDE, SIDE, ((3, 256, 512), F32)])
        + [pltpu.SemaphoreType.DMA((6,))],
        compiler_params=pltpu.CompilerParams(vmem_limit_bytes=32 * 1024 * 1024),
    )(*passed, shares, freq.reshape(6, 1), barrier.reshape(6, 1))
    return out.reshape(flow.shape), cnew, snew


def solution(mesh):
    placed = (
        P(None, "ax", "xs", None, None),
        P("ax", "xs", None, None),
        P(None, "ax", "xs", None, None),
        P("ax", "xs", None, None),
        P(None, ("ax", "xs")),
        P(None, ("ax", "xs")),
        P(("ax", "xs"), None),
        P(("ax", "xs")),
        P(None, ("ax", "xs")),
        P(),
        P(),
    )
    return jax.shard_map(
        local,
        mesh=mesh,
        in_specs=placed,
        out_specs=(P(None, "ax", "xs", None, None), P(None, ("ax", "xs")), P(None, ("ax", "xs"))),
        check_vma=False,
    )
```

```python
import functools

import jax
import jax.numpy as jnp
import numpy as np
from jax import lax
from jax.experimental import pallas as pl
from jax.experimental.pallas import tpu as pltpu
from jax.sharding import PartitionSpec as P

NODE_LIST = (
    -1.0,
    -0.8717401485096066,
    -0.5917001814331423,
    -0.2092992179024789,
    0.2092992179024789,
    0.5917001814331423,
    0.8717401485096066,
    1.0,
)
STEP_DT = 0.25
F32 = jnp.float32
BF16 = jnp.bfloat16
CHUNK = 256


def bary_weights():
    nodes = np.array(NODE_LIST)
    weights = np.zeros(8)
    for a in range(8):
        weights[a] = 1.0 / np.prod([nodes[a] - nodes[m] for m in range(8) if m != a])
    return nodes, weights


def deriv_table():
    nodes, weights = bary_weights()
    table = np.zeros((8, 8))
    for row in range(8):
        for col in range(8):
            if row != col:
                table[row, col] = weights[col] / weights[row] / (nodes[row] - nodes[col])
        table[row, row] = -np.sum(table[row])
    return table


DM = np.asarray(deriv_table(), np.float32).astype(np.float64)


def fill_tables(t_ref):
    sub = lax.broadcasted_iota(jnp.int32, (8, 128), 0)
    for half, table in enumerate((DM, DM.T)):
        for s in range(8):
            out = jnp.full((8, 128), table[0, (0 - s) % 8], F32)
            for p in range(1, 8):
                out = jnp.where(sub == p, F32(table[p, (p - s) % 8]), out)
            t_ref[half * 8 + s] = out


def apply_table(table, u):
    even = [u[i] + u[7 - i] for i in range(4)]
    odd = [u[i] - u[7 - i] for i in range(4)]
    out = [None] * 8
    for p in range(4):
        a = b = None
        for i in range(4):
            ca = float((table[p, i] + table[p, 7 - i]) / 2)
            cb = float((table[p, i] - table[p, 7 - i]) / 2)
            ta, tb = even[i] * ca, odd[i] * cb
            a = ta if a is None else a + ta
            b = tb if b is None else b + tb
        out[p], out[7 - p] = a + b, b - a
    return out


def apply_rolls(tables, x):
    y = x * tables[0]
    for s in range(1, 8):
        y = y + pltpu.roll(x, s, 0) * tables[s]
    return y


def pick_node(cell, shift):
    out = jnp.full(cell.shape, NODE_LIST[shift], F32)
    for c in range(1, 7):
        out = jnp.where(cell == c, F32(NODE_LIST[c + shift]), out)
    return out


def split(x):
    high = x.astype(BF16).astype(F32)
    return high, x - high


def dispatch(idx_ref, off_ref, own_ref, piece_ref, coords_ref, rank_ref, pay_ref):
    total = idx_ref.shape[1]
    cell = idx_ref[...]
    low, high = pick_node(cell, 0), pick_node(cell, 1)
    coords_ref[...] = low + off_ref[...] * (high - low)
    rows = lax.broadcasted_iota(jnp.int32, (CHUNK, 2 * CHUNK), 0)
    cols = lax.broadcasted_iota(jnp.int32, (CHUNK, 2 * CHUNK), 1)
    before = jnp.where((rows < cols) | (cols >= CHUNK), 1.0, 0.0).astype(BF16)
    lane_id = lax.broadcasted_iota(jnp.int32, (128, CHUNK), 0)
    base = jnp.zeros((128, CHUNK), F32)
    for c in range(total // CHUNK):
        part = pl.ds(c * CHUNK, CHUNK)
        hot = jnp.where(own_ref[:, part] == lane_id, 1.0, 0.0)
        count = jnp.dot(hot.astype(BF16), before, preferred_element_type=F32)
        rank = jnp.sum(hot * (count[:, :CHUNK] + base), axis=0, keepdims=True)
        rank_ref[:, part] = rank.astype(jnp.int32)
        base = base + count[:, CHUNK:]
    sums = [jnp.zeros((128, 128), F32)] * 4
    dims = (((1,), (1,)), ((), ()))
    for c in range(total // CHUNK):
        part = pl.ds(c * CHUNK, CHUNK)
        hot = jnp.where(own_ref[:, part] == lane_id, 1.0, 0.0).astype(BF16)
        mask = rank_ref[:, part] == lane_id
        tops, lows = [], []
        for d in range(3):
            high, rest = split(coords_ref[pl.ds(d, 1), part])
            tops.append(jnp.where(mask, high, 0.0).astype(BF16))
            lows.append(jnp.where(mask, rest, 0.0).astype(BF16))
        tops.append(jnp.where(mask, piece_ref[:, part].astype(F32), 0.0).astype(BF16))
        one = lax.dot_general(hot, jnp.concatenate(tops, 0), dims, preferred_element_type=F32)
        two = lax.dot_general(hot, jnp.concatenate(lows, 0), dims, preferred_element_type=F32)
        sums = [
            sums[v] + (one[:, v * 128 : (v + 1) * 128] + two[:, v * 128 : (v + 1) * 128] if v < 3 else one[:, 384:])
            for v in range(4)
        ]
    for v in range(4):
        pay_ref[:, v, :] = sums[v]


def interpolate(base, got_ref, table_ref, back_ref, lag_ref):
    nodes, weights = bary_weights()
    ident = lax.broadcasted_iota(jnp.int32, (256, 256), 0)
    for d in range(3):
        x = got_ref[pl.ds(base, 8), d, :]
        diff = [x - F32(n) for n in nodes]
        ahead, behind = [None] * 8, [None] * 8
        ahead[1], behind[6] = diff[0], diff[7]
        for i in range(2, 8):
            ahead[i] = ahead[i - 1] * diff[i - 1]
            behind[7 - i] = behind[8 - i] * diff[8 - i]
        for i in range(8):
            prod = behind[0] if i == 0 else ahead[7] if i == 7 else ahead[i] * behind[i]
            lag_ref[pl.ds(d * 64 + i * 8, 8), :] = prod * F32(weights[i])
    elem = got_ref[pl.ds(base, 8), 3, :].astype(jnp.int32)
    for pair in range(4):
        s0, s1 = 2 * pair, 2 * pair + 1
        ids = jnp.concatenate([elem[s0 : s0 + 1], elem[s1 : s1 + 1]], 1)
        hot = jnp.where(ident == ids, 1.0, 0.0).astype(BF16)

        def weight(d, i):
            row = d * 64 + i * 8
            return jnp.concatenate(
                [lag_ref[pl.ds(row + s0, 1), :], lag_ref[pl.ds(row + s1, 1), :]], 1
            )

        third = jnp.concatenate(
            [lag_ref[pl.ds(128 + s0, 8, stride=8), :], lag_ref[pl.ds(128 + s1, 8, stride=8), :]], 1
        )
        rows = jnp.dot(table_ref[...], hot, preferred_element_type=F32)
        for f in range(4):
            one = None
            for i in range(8):
                at = f * 512 + i * 64
                term = rows[at : at + 64] * weight(0, i)
                one = term if one is None else one + term
            two = None
            for j in range(8):
                term = one[j * 8 : (j + 1) * 8] * weight(1, j)
                two = term if two is None else two + term
            value = jnp.sum(two * third, axis=0, keepdims=True)
            back_ref[base + s0, pl.ds(f, 1), :] = value[:, :128]
            back_ref[base + s1, pl.ds(f, 1), :] = value[:, 128:]


def gather_back(ret_ref, own_ref, rank_ref, probe_ref, halves_ref):
    total = own_ref.shape[1]
    for f in range(4):
        high, rest = split(jnp.transpose(ret_ref[:, f, :]))
        halves_ref[pl.ds(f * 128, 128), 0:128] = high.astype(BF16)
        halves_ref[pl.ds(f * 128, 128), 128:256] = rest.astype(BF16)
    lane_id = lax.broadcasted_iota(jnp.int32, (128, CHUNK), 0)
    for c in range(total // CHUNK):
        part = pl.ds(c * CHUNK, CHUNK)
        hot = jnp.where(own_ref[:, part] == lane_id, 1.0, 0.0).astype(BF16)
        found = jnp.dot(
            halves_ref[...], jnp.concatenate([hot, hot], 0), preferred_element_type=F32
        )
        mask = rank_ref[:, part] == lane_id
        for f in range(4):
            kept = jnp.where(mask, found[f * 128 : (f + 1) * 128], 0.0)
            probe_ref[pl.ds(f, 1), part] = jnp.sum(kept, axis=0, keepdims=True)


def kinetics(probe_ref, coords_ref, share_ref, freq_ref, barrier_ref, cnew_ref, snew_ref):
    cnew_ref[...] = coords_ref[...] + STEP_DT * probe_ref[0:3, :]
    shares = share_ref[...]
    species = lax.broadcasted_iota(jnp.int32, shares.shape, 0)
    freq = jnp.full(shares.shape, freq_ref[0], F32)
    barrier = jnp.full(shares.shape, barrier_ref[0], F32)
    for q in range(1, 6):
        freq = jnp.where(species == q, freq_ref[q], freq)
        barrier = jnp.where(species == q, barrier_ref[q], barrier)
    rates = freq * jnp.exp(barrier * jnp.tanh(probe_ref[3:4, :] - 1.0))
    flux = rates * shares
    moved = jnp.concatenate([flux[5:6], flux[0:5]], 0)
    snew_ref[...] = shares + STEP_DT * (moved - flux)


def turn_in(flow_ref, heat_ref, stiff_ref, inert_ref, x_ref, table_ref, g_ref, c_ref):
    def three(d, carry):
        for a in range(2):
            lanes = pl.ds(a * 128, 128)
            turned = jnp.transpose(flow_ref[d, lanes, :].astype(F32))
            x_ref[d, :, lanes] = turned
            table_ref[pl.ds(pl.multiple_of(d * 512, 512), 512), lanes] = turned.astype(BF16)
            g_ref[d, :, lanes] = jnp.transpose(stiff_ref[d, lanes, :])
        return carry

    lax.fori_loop(0, 3, three, 0)
    for a in range(2):
        lanes = pl.ds(a * 128, 128)
        table_ref[pl.ds(1536, 512), lanes] = jnp.transpose(heat_ref[lanes, :].astype(F32)).astype(BF16)
        c_ref[:, lanes] = jnp.transpose(inert_ref[lanes, :])


def helm(x_ref, g_ref, c_ref, t_ref, h_ref):
    def part(n, carry):
        f, a = n // 2, n % 2
        lanes = pl.ds(pl.multiple_of(a * 128, 128), 128)
        fore = [t_ref[s] for s in range(8)]
        aft = [t_ref[8 + s] for s in range(8)]
        for i in range(8):
            at = [pl.ds(i * 64 + j * 8, 8) for j in range(8)]
            x = [x_ref[f, at[j], lanes] for j in range(8)]
            dj = apply_table(DM, x)
            dj = [g_ref[1, at[j], lanes] * dj[j] for j in range(8)]
            dj = apply_table(DM.T, dj)
            for j in range(8):
                dk = g_ref[2, at[j], lanes] * apply_rolls(fore, x[j])
                h_ref[f, at[j], lanes] = dj[j] + c_ref[at[j], lanes] * x[j] + apply_rolls(aft, dk)
        for j in range(8):
            at = [pl.ds(i * 64 + j * 8, 8) for i in range(8)]
            di = apply_table(DM, [x_ref[f, at[i], lanes] for i in range(8)])
            di = [g_ref[0, at[i], lanes] * di[i] for i in range(8)]
            di = apply_table(DM.T, di)
            for i in range(8):
                h_ref[f, at[i], lanes] += di[i]
        return carry

    lax.fori_loop(0, 6, part, 0)


def faces(h_ref, low_ref, high_ref, left_ref, right_ref):
    for f in range(3):
        low_ref[f] = h_ref[f, 0:64, 0:128]
        high_ref[f] = h_ref[f, 448:512, 128:256]
        both = h_ref[f, 448:512, 0:128] + h_ref[f, 0:64, 128:256]
        h_ref[f, 448:512, 0:128] = both
        h_ref[f, 0:64, 128:256] = both
    lane = lax.broadcasted_iota(jnp.int32, (8, 128), 1) // 32

    def pack(n, carry):
        f, a = n // 2, n % 2
        lanes = pl.ds(pl.multiple_of(a * 128, 128), 128)
        for half in range(2):
            one = two = None
            for q in range(4):
                row = (half * 4 + q) * 64
                first = h_ref[f, pl.ds(row, 8), lanes]
                last = h_ref[f, pl.ds(row + 56, 8), lanes]
                if q:
                    first = pltpu.roll(first, 32 * q, 1)
                if q < 3:
                    last = pltpu.roll(last, 32 * q + 32, 1)
                one = first if one is None else jnp.where(lane == q, first, one)
                two = last if two is None else jnp.where(lane == q, last, two)
            left_ref[f, a, half] = one
            right_ref[f, a, half] = two
        return carry

    lax.fori_loop(0, 6, pack, 0)


def radially(x):
    lane = lax.broadcasted_iota(jnp.int32, (8, 128), 1) % 32
    sub = lax.broadcasted_iota(jnp.int32, (8, 128), 0)
    up = pltpu.roll(pltpu.roll(x, 1, 1), 1, 0)
    down = pltpu.roll(pltpu.roll(x, 127, 1), 7, 0)
    x = x + jnp.where((sub == 0) & (lane != 0), up, 0.0)
    return x + jnp.where((sub == 7) & (lane != 31), down, 0.0)


def assemble_inside(h_ref, x_ref):
    def part(n, carry):
        f, a = n // 2, n % 2
        lanes = pl.ds(pl.multiple_of(a * 128, 128), 128)
        for i in range(1, 7):
            for j in range(1, 7):
                row = pl.ds(i * 64 + j * 8, 8)
                x_ref[f, row, lanes] = radially(h_ref[f, row, lanes])
        return carry

    lax.fori_loop(0, 6, part, 0)


def assemble_rim(h_ref, x_ref, low_ref, high_ref, left_ref, right_ref, corner_ref, lowest, highest):
    quarter = lax.broadcasted_iota(jnp.int32, (8, 128), 1) // 32
    under = jnp.where(lowest, F32(0.0), F32(1.0))
    over = jnp.where(highest, F32(0.0), F32(1.0))

    def near(f, carry):
        def corner(n, q, turn, scale):
            return jnp.where(quarter == q, pltpu.roll(corner_ref[n, f], turn, 1) * scale, 0.0)

        h_ref[f, 0:64, 0:128] += low_ref[f] * under
        h_ref[f, 448:512, 128:256] += high_ref[f] * over
        left_ref[f, 0, 0] += corner(0, 0, 32, under)
        left_ref[f, 1, 1] += corner(1, 3, 96, over)
        right_ref[f, 0, 0] += corner(2, 0, 32, under)
        right_ref[f, 1, 1] += corner(3, 3, 96, over)
        return carry

    lax.fori_loop(0, 3, near, 0)

    def part(n, carry):
        f, a = n // 2, n % 2
        lanes = pl.ds(pl.multiple_of(a * 128, 128), 128)
        for i in range(8):
            half, q = i // 4, i % 4
            first = h_ref[f, pl.ds(i * 64, 8), lanes]
            last = h_ref[f, pl.ds(i * 64 + 56, 8), lanes]
            before, after = left_ref[f, a, half], right_ref[f, a, half]
            if q:
                before = pltpu.roll(before, 128 - 32 * q, 1)
            if q < 3:
                after = pltpu.roll(after, 96 - 32 * q, 1)
            before = jnp.where(quarter == 0, before, pltpu.roll(last, 32, 1))
            after = jnp.where(quarter == 3, after, pltpu.roll(first, 96, 1))
            x_ref[f, pl.ds(i * 64, 8), lanes] = radially(first + before)
            x_ref[f, pl.ds(i * 64 + 56, 8), lanes] = radially(last + after)
        for i in (0, 7):
            for j in range(1, 7):
                row = pl.ds(i * 64 + j * 8, 8)
                x_ref[f, row, lanes] = radially(h_ref[f, row, lanes])
        return carry

    lax.fori_loop(0, 6, part, 0)


FIELD = ((3, 512, 256), F32)
FACE = ((3, 64, 128), F32)
SIDE = ((3, 2, 2, 8, 128), F32)
CORNER = ((4, 3, 8, 128), F32)
RIMS = [FACE, FACE, SIDE, SIDE]
SLOTS = ((128, 4, 128), F32)
MESH = pl.DeviceIdType.MESH
LIMIT = 40 * 1024 * 1024


def rim_copies(n_ax, n_xs, sent, landed, corners, send_sems, recv_sems):
    ax, xs = lax.axis_index("ax"), lax.axis_index("xs")
    low, high, left, right = sent
    plan = [
        (high, landed[0], 1, 0),
        (low, landed[1], -1, 0),
        (right, landed[2], 0, 1),
        (left, landed[3], 0, -1),
        (right.at[:, 1, 1], corners.at[0], 1, 1),
        (right.at[:, 0, 0], corners.at[1], -1, 1),
        (left.at[:, 1, 1], corners.at[2], 1, -1),
        (left.at[:, 0, 0], corners.at[3], -1, -1),
    ]
    return [
        pltpu.make_async_remote_copy(
            src_ref=src,
            dst_ref=dst,
            send_sem=send_sems.at[n],
            recv_sem=recv_sems.at[n],
            device_id=(lax.rem(ax + da + n_ax, n_ax), lax.rem(xs + dx + n_xs, n_xs)),
            device_id_type=MESH,
        )
        for n, (src, dst, da, dx) in enumerate(plan)
    ]


def main_body(n_ax, n_xs, *refs):
    (flow_h, heat_h, stiff_h, inert_h, idx_h, off_h, own_h, piece_h) = refs[:8]
    x2, probe, coords = refs[8:11]
    (flow, heat, stiff, inert, idx, off, own, piece) = refs[11:19]
    (rank, pay, got, back, ret, x, h, g, c, table, tables, lag, halves) = refs[19:32]
    (low1, high1, left1, right1, low2, high2, left2, right2, corners1) = refs[32:41]
    (low3, high3, left3, right3, low4, high4, left4, right4, corners2) = refs[41:50]
    (in_sems, out_send, out_recv, back_send, back_recv, rim_send, rim_recv) = refs[50:]
    devices = n_ax * n_xs
    ax, xs = lax.axis_index("ax"), lax.axis_index("xs")
    me = ax * n_xs + xs

    loads = [
        pltpu.make_async_copy(src, dst, in_sems.at[n])
        for n, (src, dst) in enumerate(
            zip(
                (idx_h, off_h, own_h, piece_h, flow_h, heat_h, stiff_h, inert_h),
                (idx, off, own, piece, flow, heat, stiff, inert),
            )
        )
    ]
    for load in loads:
        load.start()

    def where(n):
        return (lax.div(n, n_xs), lax.rem(n, n_xs))

    barrier = pltpu.get_barrier_semaphore()

    def greet(k, carry):
        pl.semaphore_signal(
            barrier, inc=1, device_id=where(lax.rem(me + k, devices)), device_id_type=MESH
        )
        return carry

    lax.fori_loop(1, devices, greet, 0)
    fill_tables(tables)
    for load in loads[:4]:
        load.wait()
    dispatch(idx, off, own, piece, coords, rank, pay)
    pl.semaphore_wait(barrier, devices - 1)

    group = lax.div(me, 8)
    own_copy = pltpu.make_async_copy(pay.at[me], got.at[me], out_recv.at[group])
    own_copy.start()

    def send(k, carry):
        to = lax.rem(me + k, devices)
        pltpu.make_async_remote_copy(
            src_ref=pay.at[to],
            dst_ref=got.at[me],
            send_sem=out_send,
            recv_sem=out_recv.at[group],
            device_id=where(to),
            device_id_type=MESH,
        ).start()
        return carry

    lax.fori_loop(1, devices, send, 0)

    for load in loads[4:]:
        load.wait()
    turn_in(flow, heat, stiff, inert, x, table, g, c)
    helm(x, g, c, tables, h)
    faces(h, low1, high1, left1, right1)
    first = rim_copies(
        n_ax, n_xs, (low1, high1, left1, right1), (low2, high2, left2, right2), corners1,
        rim_send.at[0], rim_recv.at[0],
    )
    for copy in first:
        copy.start()

    def block(n, carry):
        now = lax.rem(group + 2 * (devices // 8) - 1 - n, devices // 8)
        base = now * 8
        rows = got.at[pl.ds(base, 8)]
        pltpu.make_async_copy(rows, rows, out_recv.at[now]).wait()
        interpolate(base, got, table, back, lag)

        def give(s, inner):
            to = base + s

            @pl.when(to != me)
            def _():
                pltpu.make_async_remote_copy(
                    src_ref=back.at[to],
                    dst_ref=ret.at[me],
                    send_sem=back_send,
                    recv_sem=back_recv,
                    device_id=where(to),
                    device_id_type=MESH,
                ).start()

            @pl.when(to == me)
            def _():
                pltpu.make_async_copy(back.at[to], ret.at[me], back_recv).start()

            return inner

        lax.fori_loop(0, 8, give, 0)
        return carry

    lax.fori_loop(0, devices // 8, block, 0)

    assemble_inside(h, x)
    for copy in first:
        copy.wait()
    assemble_rim(h, x, low2, high2, left2, right2, corners1, ax == 0, ax == n_ax - 1)
    helm(x, g, c, tables, h)
    faces(h, low3, high3, left3, right3)
    second = rim_copies(
        n_ax, n_xs, (low3, high3, left3, right3), (low4, high4, left4, right4), corners2,
        rim_send.at[1], rim_recv.at[1],
    )
    for copy in second:
        copy.start()

    pltpu.make_async_copy(ret, ret, back_recv).wait()
    gather_back(ret, own, rank, probe, halves)
    assemble_inside(h, x2)

    others = pl.ds(0, devices - 1)
    pltpu.make_async_copy(pay.at[others], pay.at[others], out_send).wait()
    pltpu.make_async_copy(back.at[others], back.at[others], back_send).wait()
    for copy in second:
        copy.wait()
    assemble_rim(h, x2, low4, high4, left4, right4, corners2, ax == 0, ax == n_ax - 1)


def last_body(x, probe, coords, shares, freq, barrier, out, cnew, snew, turned, sems):
    copies = []
    for d in range(3):
        for a in range(2):
            lanes = pl.ds(a * 128, 128)
            turned[d, lanes, :] = jnp.transpose(x[d, :, lanes])
            copy = pltpu.make_async_copy(turned.at[d, lanes], out.at[d, lanes], sems.at[d * 2 + a])
            copy.start()
            copies.append(copy)
    kinetics(probe, coords, shares, freq, barrier, cnew, snew)
    for copy in copies:
        copy.wait()


def shapes(outs):
    return [jax.ShapeDtypeStruct(shape, dtype) for shape, dtype in outs]


def buffers(outs):
    return [pltpu.VMEM(shape, dtype) for shape, dtype in outs]


def local(flow, heat, stiff, inert, index, offset, owner, piece, shares, freq, barrier):
    particles = piece.shape[0]
    n_ax, n_xs = lax.axis_size("ax"), lax.axis_size("xs")
    devices = n_ax * n_xs
    vmem = pl.BlockSpec(memory_space=pltpu.VMEM)
    hbm = pl.BlockSpec(memory_space=pltpu.HBM)
    smem = pl.BlockSpec(memory_space=pltpu.SMEM)
    inputs = (
        flow.reshape(3, 256, 512),
        heat.reshape(256, 512),
        stiff.reshape(3, 256, 512),
        inert.reshape(256, 512),
        index,
        offset,
        owner.reshape(1, particles),
        piece.reshape(1, particles),
    )
    inputs = [pltpu.with_memory_space_constraint(a, pltpu.HBM) for a in inputs]
    held = [(a.shape, a.dtype) for a in inputs]
    table = ((2048, 256), BF16)
    outs = [FIELD, ((4, particles), F32), ((3, particles), F32)]
    passed = pl.pallas_call(
        functools.partial(main_body, n_ax, n_xs),
        out_shape=shapes(outs),
        in_specs=[hbm] * 8,
        out_specs=[vmem] * len(outs),
        scratch_shapes=buffers(held)
        + buffers([((1, particles), jnp.int32), SLOTS, SLOTS, SLOTS, SLOTS, FIELD, FIELD, FIELD])
        + buffers([((512, 256), F32), table, ((16, 8, 128), F32), ((192, 128), F32), ((512, 256), BF16)])
        + buffers([*RIMS, *RIMS, CORNER, *RIMS, *RIMS, CORNER])
        + [
            pltpu.SemaphoreType.DMA((8,)),
            pltpu.SemaphoreType.DMA,
            pltpu.SemaphoreType.DMA((devices // 8,)),
            pltpu.SemaphoreType.DMA,
            pltpu.SemaphoreType.DMA,
            pltpu.SemaphoreType.DMA((2, 8)),
            pltpu.SemaphoreType.DMA((2, 8)),
        ],
        compiler_params=pltpu.CompilerParams(
            collective_id=0, has_side_effects=True, vmem_limit_bytes=LIMIT
        ),
    )(*inputs)
    outs = [((3, 256, 512), F32), ((3, particles), F32), ((6, particles), F32)]
    out, cnew, snew = pl.pallas_call(
        last_body,
        out_shape=shapes(outs),
        in_specs=[vmem] * 4 + [smem] * 2,
        out_specs=[hbm, vmem, vmem],
        scratch_shapes=buffers([((3, 256, 512), F32)])
        + [pltpu.SemaphoreType.DMA((6,))],
        compiler_params=pltpu.CompilerParams(vmem_limit_bytes=8 * 1024 * 1024),
    )(*passed, shares, freq, barrier)
    return out.reshape(flow.shape), cnew, snew


def solution(mesh):
    placed = (
        P(None, "ax", "xs", None, None),
        P("ax", "xs", None, None),
        P(None, "ax", "xs", None, None),
        P("ax", "xs", None, None),
        P(None, ("ax", "xs")),
        P(None, ("ax", "xs")),
        P(("ax", "xs"), None),
        P(("ax", "xs")),
        P(None, ("ax", "xs")),
        P(),
        P(),
    )
    return jax.shard_map(
        local,
        mesh=mesh,
        in_specs=placed,
        out_specs=(P(None, "ax", "xs", None, None), P(None, ("ax", "xs")), P(None, ("ax", "xs"))),
        check_vma=False,
    )
```

```python
import functools

import jax
import jax.numpy as jnp
import numpy as np
from jax import lax
from jax.experimental import pallas as pl
from jax.experimental.pallas import tpu as pltpu
from jax.sharding import PartitionSpec as P

NODE_LIST = (
    -1.0,
    -0.8717401485096066,
    -0.5917001814331423,
    -0.2092992179024789,
    0.2092992179024789,
    0.5917001814331423,
    0.8717401485096066,
    1.0,
)
STEP_DT = 0.25
F32 = jnp.float32
BF16 = jnp.bfloat16
CHUNK = 256


def bary_weights():
    nodes = np.array(NODE_LIST)
    weights = np.zeros(8)
    for a in range(8):
        weights[a] = 1.0 / np.prod([nodes[a] - nodes[m] for m in range(8) if m != a])
    return nodes, weights


def deriv_table():
    nodes, weights = bary_weights()
    table = np.zeros((8, 8))
    for row in range(8):
        for col in range(8):
            if row != col:
                table[row, col] = weights[col] / weights[row] / (nodes[row] - nodes[col])
        table[row, row] = -np.sum(table[row])
    return table


DM = np.asarray(deriv_table(), np.float32).astype(np.float64)


def fill_tables(t_ref):
    sub = lax.broadcasted_iota(jnp.int32, (8, 128), 0)
    for half, table in enumerate((DM, DM.T)):
        for s in range(8):
            out = jnp.full((8, 128), table[0, (0 - s) % 8], F32)
            for p in range(1, 8):
                out = jnp.where(sub == p, F32(table[p, (p - s) % 8]), out)
            t_ref[half * 8 + s] = out


def apply_table(table, u):
    even = [u[i] + u[7 - i] for i in range(4)]
    odd = [u[i] - u[7 - i] for i in range(4)]
    out = [None] * 8
    for p in range(4):
        a = b = None
        for i in range(4):
            ca = float((table[p, i] + table[p, 7 - i]) / 2)
            cb = float((table[p, i] - table[p, 7 - i]) / 2)
            ta, tb = even[i] * ca, odd[i] * cb
            a = ta if a is None else a + ta
            b = tb if b is None else b + tb
        out[p], out[7 - p] = a + b, b - a
    return out


def apply_rolls(tables, x):
    y = x * tables[0]
    for s in range(1, 8):
        y = y + pltpu.roll(x, s, 0) * tables[s]
    return y


def pick_node(cell, shift):
    out = jnp.full(cell.shape, NODE_LIST[shift], F32)
    for c in range(1, 7):
        out = jnp.where(cell == c, F32(NODE_LIST[c + shift]), out)
    return out


def split(x):
    high = x.astype(BF16).astype(F32)
    return high, x - high


def dispatch(idx_ref, off_ref, own_ref, piece_ref, coords_ref, rank_ref, pay_ref):
    total = idx_ref.shape[1]
    cell = idx_ref[...]
    low, high = pick_node(cell, 0), pick_node(cell, 1)
    coords_ref[...] = low + off_ref[...] * (high - low)
    rows = lax.broadcasted_iota(jnp.int32, (CHUNK, 2 * CHUNK), 0)
    cols = lax.broadcasted_iota(jnp.int32, (CHUNK, 2 * CHUNK), 1)
    before = jnp.where((rows < cols) | (cols >= CHUNK), 1.0, 0.0).astype(BF16)
    lane_id = lax.broadcasted_iota(jnp.int32, (128, CHUNK), 0)
    base = jnp.zeros((128, CHUNK), F32)
    for c in range(total // CHUNK):
        part = pl.ds(c * CHUNK, CHUNK)
        hot = jnp.where(own_ref[:, part] == lane_id, 1.0, 0.0)
        count = jnp.dot(hot.astype(BF16), before, preferred_element_type=F32)
        rank = jnp.sum(hot * (count[:, :CHUNK] + base), axis=0, keepdims=True)
        rank_ref[:, part] = rank.astype(jnp.int32)
        base = base + count[:, CHUNK:]
    sums = [jnp.zeros((128, 128), F32)] * 4
    dims = (((1,), (1,)), ((), ()))
    for c in range(total // CHUNK):
        part = pl.ds(c * CHUNK, CHUNK)
        hot = jnp.where(own_ref[:, part] == lane_id, 1.0, 0.0).astype(BF16)
        mask = rank_ref[:, part] == lane_id
        tops, lows = [], []
        for d in range(3):
            high, rest = split(coords_ref[pl.ds(d, 1), part])
            tops.append(jnp.where(mask, high, 0.0).astype(BF16))
            lows.append(jnp.where(mask, rest, 0.0).astype(BF16))
        tops.append(jnp.where(mask, piece_ref[:, part].astype(F32), 0.0).astype(BF16))
        one = lax.dot_general(hot, jnp.concatenate(tops, 0), dims, preferred_element_type=F32)
        two = lax.dot_general(hot, jnp.concatenate(lows, 0), dims, preferred_element_type=F32)
        sums = [
            sums[v] + (one[:, v * 128 : (v + 1) * 128] + two[:, v * 128 : (v + 1) * 128] if v < 3 else one[:, 384:])
            for v in range(4)
        ]
    for v in range(4):
        pay_ref[:, v, :] = sums[v]


def interpolate(base, got_ref, table_ref, back_ref, lag_ref):
    nodes, weights = bary_weights()
    ident = lax.broadcasted_iota(jnp.int32, (256, 256), 0)
    for d in range(3):
        x = got_ref[pl.ds(base, 8), d, :]
        diff = [x - F32(n) for n in nodes]
        ahead, behind = [None] * 8, [None] * 8
        ahead[1], behind[6] = diff[0], diff[7]
        for i in range(2, 8):
            ahead[i] = ahead[i - 1] * diff[i - 1]
            behind[7 - i] = behind[8 - i] * diff[8 - i]
        for i in range(8):
            prod = behind[0] if i == 0 else ahead[7] if i == 7 else ahead[i] * behind[i]
            lag_ref[pl.ds(d * 64 + i * 8, 8), :] = prod * F32(weights[i])
    elem = got_ref[pl.ds(base, 8), 3, :].astype(jnp.int32)
    for pair in range(4):
        s0, s1 = 2 * pair, 2 * pair + 1
        ids = jnp.concatenate([elem[s0 : s0 + 1], elem[s1 : s1 + 1]], 1)
        hot = jnp.where(ident == ids, 1.0, 0.0).astype(BF16)

        def weight(d, i):
            row = d * 64 + i * 8
            return jnp.concatenate(
                [lag_ref[pl.ds(row + s0, 1), :], lag_ref[pl.ds(row + s1, 1), :]], 1
            )

        third = jnp.concatenate(
            [lag_ref[pl.ds(128 + s0, 8, stride=8), :], lag_ref[pl.ds(128 + s1, 8, stride=8), :]], 1
        )
        rows = jnp.dot(table_ref[...], hot, preferred_element_type=F32)
        for f in range(4):
            one = None
            for i in range(8):
                at = f * 512 + i * 64
                term = rows[at : at + 64] * weight(0, i)
                one = term if one is None else one + term
            two = None
            for j in range(8):
                term = one[j * 8 : (j + 1) * 8] * weight(1, j)
                two = term if two is None else two + term
            value = jnp.sum(two * third, axis=0, keepdims=True)
            back_ref[base + s0, pl.ds(f, 1), :] = value[:, :128]
            back_ref[base + s1, pl.ds(f, 1), :] = value[:, 128:]


def gather_back(ret_ref, own_ref, rank_ref, probe_ref, halves_ref):
    total = own_ref.shape[1]
    for f in range(4):
        high, rest = split(jnp.transpose(ret_ref[:, f, :]))
        halves_ref[pl.ds(f * 128, 128), 0:128] = high.astype(BF16)
        halves_ref[pl.ds(f * 128, 128), 128:256] = rest.astype(BF16)
    lane_id = lax.broadcasted_iota(jnp.int32, (128, CHUNK), 0)
    for c in range(total // CHUNK):
        part = pl.ds(c * CHUNK, CHUNK)
        hot = jnp.where(own_ref[:, part] == lane_id, 1.0, 0.0).astype(BF16)
        found = jnp.dot(
            halves_ref[...], jnp.concatenate([hot, hot], 0), preferred_element_type=F32
        )
        mask = rank_ref[:, part] == lane_id
        for f in range(4):
            kept = jnp.where(mask, found[f * 128 : (f + 1) * 128], 0.0)
            probe_ref[pl.ds(f, 1), part] = jnp.sum(kept, axis=0, keepdims=True)


def kinetics(probe_ref, coords_ref, share_ref, freq_ref, barrier_ref, cnew_ref, snew_ref):
    cnew_ref[...] = coords_ref[...] + STEP_DT * probe_ref[0:3, :]
    shares = share_ref[...]
    species = lax.broadcasted_iota(jnp.int32, shares.shape, 0)
    freq = jnp.full(shares.shape, freq_ref[0], F32)
    barrier = jnp.full(shares.shape, barrier_ref[0], F32)
    for q in range(1, 6):
        freq = jnp.where(species == q, freq_ref[q], freq)
        barrier = jnp.where(species == q, barrier_ref[q], barrier)
    rates = freq * jnp.exp(barrier * jnp.tanh(probe_ref[3:4, :] - 1.0))
    flux = rates * shares
    moved = jnp.concatenate([flux[5:6], flux[0:5]], 0)
    snew_ref[...] = shares + STEP_DT * (moved - flux)


def turn_in(flow_ref, heat_ref, stiff_ref, inert_ref, x_ref, table_ref, g_ref, c_ref):
    def three(d, carry):
        for a in range(2):
            lanes = pl.ds(a * 128, 128)
            turned = jnp.transpose(flow_ref[d, lanes, :].astype(F32))
            x_ref[d, :, lanes] = turned
            table_ref[pl.ds(pl.multiple_of(d * 512, 512), 512), lanes] = turned.astype(BF16)
            g_ref[d, :, lanes] = jnp.transpose(stiff_ref[d, lanes, :])
        return carry

    lax.fori_loop(0, 3, three, 0)
    for a in range(2):
        lanes = pl.ds(a * 128, 128)
        table_ref[pl.ds(1536, 512), lanes] = jnp.transpose(heat_ref[lanes, :].astype(F32)).astype(BF16)
        c_ref[:, lanes] = jnp.transpose(inert_ref[lanes, :])


def helm(x_ref, g_ref, c_ref, t_ref, h_ref):
    def part(n, carry):
        f, a = n // 2, n % 2
        lanes = pl.ds(pl.multiple_of(a * 128, 128), 128)
        fore = [t_ref[s] for s in range(8)]
        aft = [t_ref[8 + s] for s in range(8)]
        for i in range(8):
            at = [pl.ds(i * 64 + j * 8, 8) for j in range(8)]
            x = [x_ref[f, at[j], lanes] for j in range(8)]
            dj = apply_table(DM, x)
            dj = [g_ref[1, at[j], lanes] * dj[j] for j in range(8)]
            dj = apply_table(DM.T, dj)
            for j in range(8):
                dk = g_ref[2, at[j], lanes] * apply_rolls(fore, x[j])
                h_ref[f, at[j], lanes] = dj[j] + c_ref[at[j], lanes] * x[j] + apply_rolls(aft, dk)
        for j in range(8):
            at = [pl.ds(i * 64 + j * 8, 8) for i in range(8)]
            di = apply_table(DM, [x_ref[f, at[i], lanes] for i in range(8)])
            di = [g_ref[0, at[i], lanes] * di[i] for i in range(8)]
            di = apply_table(DM.T, di)
            for i in range(8):
                h_ref[f, at[i], lanes] += di[i]
        return carry

    lax.fori_loop(0, 6, part, 0)


def faces(h_ref, low_ref, high_ref, left_ref, right_ref):
    for f in range(3):
        low_ref[f] = h_ref[f, 0:64, 0:128]
        high_ref[f] = h_ref[f, 448:512, 128:256]
        both = h_ref[f, 448:512, 0:128] + h_ref[f, 0:64, 128:256]
        h_ref[f, 448:512, 0:128] = both
        h_ref[f, 0:64, 128:256] = both
    lane = lax.broadcasted_iota(jnp.int32, (8, 128), 1) // 32

    def pack(n, carry):
        f, a = n // 2, n % 2
        lanes = pl.ds(pl.multiple_of(a * 128, 128), 128)
        for half in range(2):
            one = two = None
            for q in range(4):
                row = (half * 4 + q) * 64
                first = h_ref[f, pl.ds(row, 8), lanes]
                last = h_ref[f, pl.ds(row + 56, 8), lanes]
                if q:
                    first = pltpu.roll(first, 32 * q, 1)
                if q < 3:
                    last = pltpu.roll(last, 32 * q + 32, 1)
                one = first if one is None else jnp.where(lane == q, first, one)
                two = last if two is None else jnp.where(lane == q, last, two)
            left_ref[f, a, half] = one
            right_ref[f, a, half] = two
        return carry

    lax.fori_loop(0, 6, pack, 0)


def radially(x):
    lane = lax.broadcasted_iota(jnp.int32, (8, 128), 1) % 32
    sub = lax.broadcasted_iota(jnp.int32, (8, 128), 0)
    up = pltpu.roll(pltpu.roll(x, 1, 1), 1, 0)
    down = pltpu.roll(pltpu.roll(x, 127, 1), 7, 0)
    x = x + jnp.where((sub == 0) & (lane != 0), up, 0.0)
    return x + jnp.where((sub == 7) & (lane != 31), down, 0.0)


def assemble_inside(h_ref, x_ref):
    def part(n, carry):
        f, a = n // 2, n % 2
        lanes = pl.ds(pl.multiple_of(a * 128, 128), 128)
        for i in range(1, 7):
            for j in range(1, 7):
                row = pl.ds(i * 64 + j * 8, 8)
                x_ref[f, row, lanes] = radially(h_ref[f, row, lanes])
        return carry

    lax.fori_loop(0, 6, part, 0)


def assemble_rim(h_ref, x_ref, low_ref, high_ref, left_ref, right_ref, corner_ref, lowest, highest):
    quarter = lax.broadcasted_iota(jnp.int32, (8, 128), 1) // 32
    under = jnp.where(lowest, F32(0.0), F32(1.0))
    over = jnp.where(highest, F32(0.0), F32(1.0))

    def near(f, carry):
        def corner(n, q, turn, scale):
            return jnp.where(quarter == q, pltpu.roll(corner_ref[n, f], turn, 1) * scale, 0.0)

        h_ref[f, 0:64, 0:128] += low_ref[f] * under
        h_ref[f, 448:512, 128:256] += high_ref[f] * over
        left_ref[f, 0, 0] += corner(0, 0, 32, under)
        left_ref[f, 1, 1] += corner(1, 3, 96, over)
        right_ref[f, 0, 0] += corner(2, 0, 32, under)
        right_ref[f, 1, 1] += corner(3, 3, 96, over)
        return carry

    lax.fori_loop(0, 3, near, 0)

    def part(n, carry):
        f, a = n // 2, n % 2
        lanes = pl.ds(pl.multiple_of(a * 128, 128), 128)
        for i in range(8):
            half, q = i // 4, i % 4
            first = h_ref[f, pl.ds(i * 64, 8), lanes]
            last = h_ref[f, pl.ds(i * 64 + 56, 8), lanes]
            before, after = left_ref[f, a, half], right_ref[f, a, half]
            if q:
                before = pltpu.roll(before, 128 - 32 * q, 1)
            if q < 3:
                after = pltpu.roll(after, 96 - 32 * q, 1)
            before = jnp.where(quarter == 0, before, pltpu.roll(last, 32, 1))
            after = jnp.where(quarter == 3, after, pltpu.roll(first, 96, 1))
            x_ref[f, pl.ds(i * 64, 8), lanes] = radially(first + before)
            x_ref[f, pl.ds(i * 64 + 56, 8), lanes] = radially(last + after)
        for i in (0, 7):
            for j in range(1, 7):
                row = pl.ds(i * 64 + j * 8, 8)
                x_ref[f, row, lanes] = radially(h_ref[f, row, lanes])
        return carry

    lax.fori_loop(0, 6, part, 0)


def turn_out(x_ref, out_ref):
    def three(d, carry):
        for a in range(2):
            lanes = pl.ds(a * 128, 128)
            out_ref[d, lanes, :] = jnp.transpose(x_ref[d, :, lanes])
        return carry

    lax.fori_loop(0, 3, three, 0)


FIELD = ((3, 512, 256), F32)
FACE = ((3, 64, 128), F32)
SIDE = ((3, 2, 2, 8, 128), F32)
CORNER = ((4, 3, 8, 128), F32)
RIMS = [FACE, FACE, SIDE, SIDE]
SLOTS = ((128, 4, 128), F32)
MESH = pl.DeviceIdType.MESH
LIMIT = 40 * 1024 * 1024


def rim_copies(n_ax, n_xs, sent, landed, corners, send_sems, recv_sems):
    ax, xs = lax.axis_index("ax"), lax.axis_index("xs")
    low, high, left, right = sent
    plan = [
        (high, landed[0], 1, 0),
        (low, landed[1], -1, 0),
        (right, landed[2], 0, 1),
        (left, landed[3], 0, -1),
        (right.at[:, 1, 1], corners.at[0], 1, 1),
        (right.at[:, 0, 0], corners.at[1], -1, 1),
        (left.at[:, 1, 1], corners.at[2], 1, -1),
        (left.at[:, 0, 0], corners.at[3], -1, -1),
    ]
    return [
        pltpu.make_async_remote_copy(
            src_ref=src,
            dst_ref=dst,
            send_sem=send_sems.at[n],
            recv_sem=recv_sems.at[n],
            device_id=(lax.rem(ax + da + n_ax, n_ax), lax.rem(xs + dx + n_xs, n_xs)),
            device_id_type=MESH,
        )
        for n, (src, dst, da, dx) in enumerate(plan)
    ]


def main_body(n_ax, n_xs, *refs):
    (flow_h, heat_h, stiff_h, inert_h, idx_h, off_h, own_h, piece_h) = refs[:8]
    turned, probe, coords = refs[8:11]
    (flow, heat, stiff, inert, idx, off, own, piece) = refs[11:19]
    (rank, pay, got, back, ret, x, h, g, c, table, tables, lag, halves) = refs[19:32]
    (low1, high1, left1, right1, low2, high2, left2, right2, corners1) = refs[32:41]
    (low3, high3, left3, right3, low4, high4, left4, right4, corners2) = refs[41:50]
    (in_sems, out_send, out_recv, back_send, back_recv, rim_send, rim_recv) = refs[50:]
    devices = n_ax * n_xs
    ax, xs = lax.axis_index("ax"), lax.axis_index("xs")
    me = ax * n_xs + xs

    loads = [
        pltpu.make_async_copy(src, dst, in_sems.at[n])
        for n, (src, dst) in enumerate(
            zip(
                (idx_h, off_h, own_h, piece_h, flow_h, heat_h, stiff_h, inert_h),
                (idx, off, own, piece, flow, heat, stiff, inert),
            )
        )
    ]
    for load in loads:
        load.start()

    def where(n):
        return (lax.div(n, n_xs), lax.rem(n, n_xs))

    barrier = pltpu.get_barrier_semaphore()

    def greet(k, carry):
        pl.semaphore_signal(
            barrier, inc=1, device_id=where(lax.rem(me + k, devices)), device_id_type=MESH
        )
        return carry

    lax.fori_loop(1, devices, greet, 0)
    fill_tables(tables)
    for load in loads[:4]:
        load.wait()
    dispatch(idx, off, own, piece, coords, rank, pay)
    pl.semaphore_wait(barrier, devices - 1)

    own_copy = pltpu.make_async_copy(pay.at[me], got.at[me], out_recv.at[ax])
    own_copy.start()

    def send(k, carry):
        to = lax.rem(me + k, devices)
        pltpu.make_async_remote_copy(
            src_ref=pay.at[to],
            dst_ref=got.at[me],
            send_sem=out_send,
            recv_sem=out_recv.at[ax],
            device_id=where(to),
            device_id_type=MESH,
        ).start()
        return carry

    lax.fori_loop(1, devices, send, 0)

    for load in loads[4:]:
        load.wait()
    turn_in(flow, heat, stiff, inert, x, table, g, c)
    helm(x, g, c, tables, h)
    faces(h, low1, high1, left1, right1)
    first = rim_copies(
        n_ax, n_xs, (low1, high1, left1, right1), (low2, high2, left2, right2), corners1,
        rim_send.at[0], rim_recv.at[0],
    )
    for copy in first:
        copy.start()

    def block(n, carry):
        now = lax.rem(ax + 2 * n_ax - 1 - n, n_ax)
        base = now * n_xs
        rows = got.at[pl.ds(base, n_xs)]
        pltpu.make_async_copy(rows, rows, out_recv.at[now]).wait()
        for part in range(n_xs // 8):
            interpolate(base + part * 8, got, table, back, lag.at[part])

        def give(s, inner):
            to = base + s

            @pl.when(to != me)
            def _():
                pltpu.make_async_remote_copy(
                    src_ref=back.at[to],
                    dst_ref=ret.at[me],
                    send_sem=back_send,
                    recv_sem=back_recv,
                    device_id=(now, s),
                    device_id_type=MESH,
                ).start()

            @pl.when(to == me)
            def _():
                pltpu.make_async_copy(back.at[to], ret.at[me], back_recv).start()

            return inner

        lax.fori_loop(0, n_xs, give, 0)
        return carry

    lax.fori_loop(0, n_ax // 4, block, 0)
    assemble_inside(h, x)
    for copy in first:
        copy.wait()
    assemble_rim(h, x, low2, high2, left2, right2, corners1, ax == 0, ax == n_ax - 1)
    helm(x, g, c, tables, h)
    faces(h, low3, high3, left3, right3)
    second = rim_copies(
        n_ax, n_xs, (low3, high3, left3, right3), (low4, high4, left4, right4), corners2,
        rim_send.at[1], rim_recv.at[1],
    )
    for copy in second:
        copy.start()
    lax.fori_loop(n_ax // 4, n_ax, block, 0)

    assemble_inside(h, x)
    for copy in second:
        copy.wait()
    assemble_rim(h, x, low4, high4, left4, right4, corners2, ax == 0, ax == n_ax - 1)
    turn_out(x, turned)
    pltpu.make_async_copy(ret, ret, back_recv).wait()
    gather_back(ret, own, rank, probe, halves)

    others = pl.ds(0, devices - 1)
    pltpu.make_async_copy(pay.at[others], pay.at[others], out_send).wait()
    pltpu.make_async_copy(back.at[others], back.at[others], back_send).wait()


def last_body(turned, probe, coords, shares, freq, barrier, out, cnew, snew, sem):
    copy = pltpu.make_async_copy(turned, out, sem)
    copy.start()
    kinetics(probe, coords, shares, freq, barrier, cnew, snew)
    copy.wait()


def shapes(outs):
    return [jax.ShapeDtypeStruct(shape, dtype) for shape, dtype in outs]


def buffers(outs):
    return [pltpu.VMEM(shape, dtype) for shape, dtype in outs]


def local(flow, heat, stiff, inert, index, offset, owner, piece, shares, freq, barrier):
    particles = piece.shape[0]
    n_ax, n_xs = lax.axis_size("ax"), lax.axis_size("xs")
    devices = n_ax * n_xs
    vmem = pl.BlockSpec(memory_space=pltpu.VMEM)
    hbm = pl.BlockSpec(memory_space=pltpu.HBM)
    smem = pl.BlockSpec(memory_space=pltpu.SMEM)
    inputs = (
        flow.reshape(3, 256, 512),
        heat.reshape(256, 512),
        stiff.reshape(3, 256, 512),
        inert.reshape(256, 512),
        index,
        offset,
        owner.reshape(1, particles),
        piece.reshape(1, particles),
    )
    inputs = [pltpu.with_memory_space_constraint(a, pltpu.HBM) for a in inputs]
    held = [(a.shape, a.dtype) for a in inputs]
    table = ((2048, 256), BF16)
    outs = [((3, 256, 512), F32), ((4, particles), F32), ((3, particles), F32)]
    passed = pl.pallas_call(
        functools.partial(main_body, n_ax, n_xs),
        out_shape=shapes(outs),
        in_specs=[hbm] * 8,
        out_specs=[vmem] * len(outs),
        scratch_shapes=buffers(held)
        + buffers([((1, particles), jnp.int32), SLOTS, SLOTS, SLOTS, SLOTS, FIELD, FIELD, FIELD])
        + buffers([((512, 256), F32), table, ((16, 8, 128), F32), ((2, 192, 128), F32), ((512, 256), BF16)])
        + buffers([*RIMS, *RIMS, CORNER, *RIMS, *RIMS, CORNER])
        + [
            pltpu.SemaphoreType.DMA((8,)),
            pltpu.SemaphoreType.DMA,
            pltpu.SemaphoreType.DMA((n_ax,)),
            pltpu.SemaphoreType.DMA,
            pltpu.SemaphoreType.DMA,
            pltpu.SemaphoreType.DMA((2, 8)),
            pltpu.SemaphoreType.DMA((2, 8)),
        ],
        compiler_params=pltpu.CompilerParams(
            collective_id=0, has_side_effects=True, vmem_limit_bytes=LIMIT
        ),
    )(*inputs)
    outs = [((3, 256, 512), F32), ((3, particles), F32), ((6, particles), F32)]
    out, cnew, snew = pl.pallas_call(
        last_body,
        out_shape=shapes(outs),
        in_specs=[vmem] * 4 + [smem] * 2,
        out_specs=[hbm, vmem, vmem],
        scratch_shapes=[pltpu.SemaphoreType.DMA],
        compiler_params=pltpu.CompilerParams(vmem_limit_bytes=8 * 1024 * 1024),
    )(*passed, shares, freq, barrier)
    return out.reshape(flow.shape), cnew, snew


def solution(mesh):
    placed = (
        P(None, "ax", "xs", None, None),
        P("ax", "xs", None, None),
        P(None, "ax", "xs", None, None),
        P("ax", "xs", None, None),
        P(None, ("ax", "xs")),
        P(None, ("ax", "xs")),
        P(("ax", "xs"), None),
        P(("ax", "xs")),
        P(None, ("ax", "xs")),
        P(),
        P(),
    )
    return jax.shard_map(
        local,
        mesh=mesh,
        in_specs=placed,
        out_specs=(P(None, "ax", "xs", None, None), P(None, ("ax", "xs")), P(None, ("ax", "xs"))),
        check_vma=False,
    )
```

```python
import functools

import jax
import jax.numpy as jnp
import numpy as np
from jax import lax
from jax.experimental import pallas as pl
from jax.experimental.pallas import tpu as pltpu
from jax.sharding import PartitionSpec as P

NODE_LIST = (
    -1.0,
    -0.8717401485096066,
    -0.5917001814331423,
    -0.2092992179024789,
    0.2092992179024789,
    0.5917001814331423,
    0.8717401485096066,
    1.0,
)
STEP_DT = 0.25
F32 = jnp.float32
BF16 = jnp.bfloat16
CHUNK = 256


def bary_weights():
    nodes = np.array(NODE_LIST)
    weights = np.zeros(8)
    for a in range(8):
        weights[a] = 1.0 / np.prod([nodes[a] - nodes[m] for m in range(8) if m != a])
    return nodes, weights


def deriv_table():
    nodes, weights = bary_weights()
    table = np.zeros((8, 8))
    for row in range(8):
        for col in range(8):
            if row != col:
                table[row, col] = weights[col] / weights[row] / (nodes[row] - nodes[col])
        table[row, row] = -np.sum(table[row])
    return table


DM = np.asarray(deriv_table(), np.float32).astype(np.float64)


def apply_table(table, u):
    even = [u[i] + u[7 - i] for i in range(4)]
    odd = [u[i] - u[7 - i] for i in range(4)]
    out = [None] * 8
    for p in range(4):
        a = b = None
        for i in range(4):
            ca = float((table[p, i] + table[p, 7 - i]) / 2)
            cb = float((table[p, i] - table[p, 7 - i]) / 2)
            ta, tb = even[i] * ca, odd[i] * cb
            a = ta if a is None else a + ta
            b = tb if b is None else b + tb
        out[p], out[7 - p] = a + b, b - a
    return out


def pick_node(cell, shift):
    out = jnp.full(cell.shape, NODE_LIST[shift], F32)
    for c in range(1, 7):
        out = jnp.where(cell == c, F32(NODE_LIST[c + shift]), out)
    return out


def split(x):
    high = x.astype(BF16).astype(F32)
    return high, x - high


def dispatch(idx_ref, off_ref, own_ref, piece_ref, coords_ref, rank_ref, pay_ref):
    total = idx_ref.shape[1]
    cell = idx_ref[...]
    low, high = pick_node(cell, 0), pick_node(cell, 1)
    coords_ref[...] = low + off_ref[...] * (high - low)
    rows = lax.broadcasted_iota(jnp.int32, (CHUNK, 2 * CHUNK), 0)
    cols = lax.broadcasted_iota(jnp.int32, (CHUNK, 2 * CHUNK), 1)
    before = jnp.where((rows < cols) | (cols >= CHUNK), 1.0, 0.0).astype(BF16)
    lane_id = lax.broadcasted_iota(jnp.int32, (128, CHUNK), 0)
    base = jnp.zeros((128, CHUNK), F32)
    for c in range(total // CHUNK):
        part = pl.ds(c * CHUNK, CHUNK)
        hot = jnp.where(own_ref[:, part] == lane_id, 1.0, 0.0)
        count = jnp.dot(hot.astype(BF16), before, preferred_element_type=F32)
        rank = jnp.sum(hot * (count[:, :CHUNK] + base), axis=0, keepdims=True)
        rank_ref[:, part] = rank.astype(jnp.int32)
        base = base + count[:, CHUNK:]
    sums = [jnp.zeros((128, 128), F32)] * 4
    dims = (((1,), (1,)), ((), ()))
    for c in range(total // CHUNK):
        part = pl.ds(c * CHUNK, CHUNK)
        hot = jnp.where(own_ref[:, part] == lane_id, 1.0, 0.0).astype(BF16)
        mask = rank_ref[:, part] == lane_id
        tops, lows = [], []
        for d in range(3):
            high, rest = split(coords_ref[pl.ds(d, 1), part])
            tops.append(jnp.where(mask, high, 0.0).astype(BF16))
            lows.append(jnp.where(mask, rest, 0.0).astype(BF16))
        tops.append(jnp.where(mask, piece_ref[:, part].astype(F32), 0.0).astype(BF16))
        one = lax.dot_general(hot, jnp.concatenate(tops, 0), dims, preferred_element_type=F32)
        two = lax.dot_general(hot, jnp.concatenate(lows, 0), dims, preferred_element_type=F32)
        sums = [
            sums[v] + (one[:, v * 128 : (v + 1) * 128] + two[:, v * 128 : (v + 1) * 128] if v < 3 else one[:, 384:])
            for v in range(4)
        ]
    for v in range(4):
        pay_ref[:, v, :] = sums[v]


def interpolate(base, got_ref, table_ref, back_ref, lag_ref):
    nodes, weights = bary_weights()
    ident = lax.broadcasted_iota(jnp.int32, (256, 256), 0)
    for d in range(3):
        x = got_ref[pl.ds(base, 8), d, :]
        diff = [x - F32(n) for n in nodes]
        ahead, behind = [None] * 8, [None] * 8
        ahead[1], behind[6] = diff[0], diff[7]
        for i in range(2, 8):
            ahead[i] = ahead[i - 1] * diff[i - 1]
            behind[7 - i] = behind[8 - i] * diff[8 - i]
        for i in range(8):
            prod = behind[0] if i == 0 else ahead[7] if i == 7 else ahead[i] * behind[i]
            lag_ref[pl.ds(d * 64 + i * 8, 8), :] = prod * F32(weights[i])
    elem = got_ref[pl.ds(base, 8), 3, :].astype(jnp.int32)
    for pair in range(4):
        s0, s1 = 2 * pair, 2 * pair + 1
        ids = jnp.concatenate([elem[s0 : s0 + 1], elem[s1 : s1 + 1]], 1)
        hot = jnp.where(ident == ids, 1.0, 0.0).astype(BF16)

        def weight(d, i):
            row = d * 64 + i * 8
            return jnp.concatenate(
                [lag_ref[pl.ds(row + s0, 1), :], lag_ref[pl.ds(row + s1, 1), :]], 1
            )

        third = jnp.concatenate(
            [lag_ref[pl.ds(128 + s0, 8, stride=8), :], lag_ref[pl.ds(128 + s1, 8, stride=8), :]], 1
        )
        rows = jnp.dot(table_ref[...], hot, preferred_element_type=F32)
        for f in range(4):
            one = None
            for i in range(8):
                at = f * 512 + i * 64
                term = rows[at : at + 64] * weight(0, i)
                one = term if one is None else one + term
            two = None
            for j in range(8):
                term = one[j * 8 : (j + 1) * 8] * weight(1, j)
                two = term if two is None else two + term
            value = jnp.sum(two * third, axis=0, keepdims=True)
            back_ref[base + s0, pl.ds(f, 1), :] = value[:, :128]
            back_ref[base + s1, pl.ds(f, 1), :] = value[:, 128:]


def gather_back(ret_ref, own_ref, rank_ref, probe_ref, halves_ref):
    total = own_ref.shape[1]
    for f in range(4):
        high, rest = split(jnp.transpose(ret_ref[:, f, :]))
        halves_ref[pl.ds(f * 128, 128), 0:128] = high.astype(BF16)
        halves_ref[pl.ds(f * 128, 128), 128:256] = rest.astype(BF16)
    lane_id = lax.broadcasted_iota(jnp.int32, (128, CHUNK), 0)
    for c in range(total // CHUNK):
        part = pl.ds(c * CHUNK, CHUNK)
        hot = jnp.where(own_ref[:, part] == lane_id, 1.0, 0.0).astype(BF16)
        found = jnp.dot(
            halves_ref[...], jnp.concatenate([hot, hot], 0), preferred_element_type=F32
        )
        mask = rank_ref[:, part] == lane_id
        for f in range(4):
            kept = jnp.where(mask, found[f * 128 : (f + 1) * 128], 0.0)
            probe_ref[pl.ds(f, 1), part] = jnp.sum(kept, axis=0, keepdims=True)


def kinetics(probe_ref, coords_ref, share_ref, freq_ref, barrier_ref, cnew_ref, snew_ref):
    cnew_ref[...] = coords_ref[...] + STEP_DT * probe_ref[0:3, :]
    shares = share_ref[...]
    species = lax.broadcasted_iota(jnp.int32, shares.shape, 0)
    freq = jnp.full(shares.shape, freq_ref[0], F32)
    barrier = jnp.full(shares.shape, barrier_ref[0], F32)
    for q in range(1, 6):
        freq = jnp.where(species == q, freq_ref[q], freq)
        barrier = jnp.where(species == q, barrier_ref[q], barrier)
    rates = freq * jnp.exp(barrier * jnp.tanh(probe_ref[3:4, :] - 1.0))
    flux = rates * shares
    moved = jnp.concatenate([flux[5:6], flux[0:5]], 0)
    snew_ref[...] = shares + STEP_DT * (moved - flux)


def turn_in(flow_ref, heat_ref, stiff_ref, inert_ref, x_ref, table_ref, g_ref, c_ref):
    def three(d, carry):
        for a in range(2):
            lanes = pl.ds(a * 128, 128)
            turned = jnp.transpose(flow_ref[d, lanes, :].astype(F32))
            x_ref[d * 2 + a] = turned
            table_ref[pl.ds(pl.multiple_of(d * 512, 512), 512), lanes] = turned.astype(BF16)
            g_ref[d * 2 + a] = jnp.transpose(stiff_ref[d, lanes, :])
        return carry

    lax.fori_loop(0, 3, three, 0)
    for a in range(2):
        lanes = pl.ds(a * 128, 128)
        table_ref[pl.ds(1536, 512), lanes] = jnp.transpose(heat_ref[lanes, :].astype(F32)).astype(BF16)
        c_ref[a] = jnp.transpose(inert_ref[lanes, :])


def helm(x_ref, g_ref, c_ref, h_ref):
    def part(n, carry):
        a = n % 2

        def along(d, at):
            line = apply_table(DM, [x_ref[n, p, :] for p in at])
            return apply_table(DM.T, [g_ref[d * 2 + a, at[p], :] * line[p] for p in range(8)])

        for i in range(8):
            at = [pl.ds(i * 64 + j * 8, 8) for j in range(8)]
            line = along(1, at)
            for j in range(8):
                h_ref[n, at[j], :] = line[j] + c_ref[a, at[j], :] * x_ref[n, at[j], :]
        for j in range(8):
            at = [pl.ds(i * 64 + j * 8, 8) for i in range(8)]
            line = along(0, at)
            for i in range(8):
                h_ref[n, at[i], :] += line[i]
        for i in range(8):
            at = [pl.ds(i * 64 + k, 8, stride=8) for k in range(8)]
            line = along(2, at)
            for k in range(8):
                h_ref[n, at[k], :] += line[k]
        return carry

    lax.fori_loop(0, 6, part, 0)


def faces(h_ref, low_ref, high_ref, left_ref, right_ref):
    for f in range(3):
        low_ref[f] = h_ref[2 * f, 0:64]
        high_ref[f] = h_ref[2 * f + 1, 448:512]
        both = h_ref[2 * f, 448:512] + h_ref[2 * f + 1, 0:64]
        h_ref[2 * f, 448:512] = both
        h_ref[2 * f + 1, 0:64] = both
    lane = lax.broadcasted_iota(jnp.int32, (8, 128), 1) // 32

    def pack(n, carry):
        f, a = n // 2, n % 2
        for half in range(2):
            one = two = None
            for q in range(4):
                row = (half * 4 + q) * 64
                first = h_ref[n, pl.ds(row, 8), :]
                last = h_ref[n, pl.ds(row + 56, 8), :]
                if q:
                    first = pltpu.roll(first, 32 * q, 1)
                if q < 3:
                    last = pltpu.roll(last, 32 * q + 32, 1)
                one = first if one is None else jnp.where(lane == q, first, one)
                two = last if two is None else jnp.where(lane == q, last, two)
            left_ref[f, a, half] = one
            right_ref[f, a, half] = two
        return carry

    lax.fori_loop(0, 6, pack, 0)


def assemble(h_ref, low_ref, high_ref, left_ref, right_ref, corner_ref, lowest, highest):
    lane = lax.broadcasted_iota(jnp.int32, (8, 128), 1)
    quarter, radial = lane // 32, lane % 32
    under = jnp.where(lowest, F32(0.0), F32(1.0))
    over = jnp.where(highest, F32(0.0), F32(1.0))

    def near(f, carry):
        def corner(n, q, turn, scale):
            return jnp.where(quarter == q, pltpu.roll(corner_ref[n, f], turn, 1) * scale, 0.0)

        h_ref[2 * f, 0:64] += low_ref[f] * under
        h_ref[2 * f + 1, 448:512] += high_ref[f] * over
        left_ref[f, 0, 0] += corner(0, 0, 32, under)
        left_ref[f, 1, 1] += corner(1, 3, 96, over)
        right_ref[f, 0, 0] += corner(2, 0, 32, under)
        right_ref[f, 1, 1] += corner(3, 3, 96, over)
        return carry

    lax.fori_loop(0, 3, near, 0)

    def part(n, carry):
        f, a = n // 2, n % 2
        for i in range(8):
            half, q = i // 4, i % 4
            first = h_ref[n, pl.ds(i * 64, 8), :]
            last = h_ref[n, pl.ds(i * 64 + 56, 8), :]
            before, after = left_ref[f, a, half], right_ref[f, a, half]
            if q:
                before = pltpu.roll(before, 128 - 32 * q, 1)
            if q < 3:
                after = pltpu.roll(after, 96 - 32 * q, 1)
            before = jnp.where(quarter == 0, before, pltpu.roll(last, 32, 1))
            after = jnp.where(quarter == 3, after, pltpu.roll(first, 96, 1))
            h_ref[n, pl.ds(i * 64, 8), :] = first + before
            h_ref[n, pl.ds(i * 64 + 56, 8), :] = last + after
        for i in range(8):
            inner, outer = pl.ds(i * 64, 8, stride=8), pl.ds(i * 64 + 7, 8, stride=8)
            first, last = h_ref[n, inner, :], h_ref[n, outer, :]
            h_ref[n, inner, :] = first + jnp.where(radial != 0, pltpu.roll(last, 1, 1), 0.0)
            h_ref[n, outer, :] = last + jnp.where(radial != 31, pltpu.roll(first, 127, 1), 0.0)
        return carry

    lax.fori_loop(0, 6, part, 0)


def turn_out(x_ref, out_ref):
    def three(d, carry):
        for a in range(2):
            lanes = pl.ds(a * 128, 128)
            out_ref[d, lanes, :] = jnp.transpose(x_ref[d * 2 + a])
        return carry

    lax.fori_loop(0, 3, three, 0)


FIELD = ((6, 512, 128), F32)
FACE = ((3, 64, 128), F32)
SIDE = ((3, 2, 2, 8, 128), F32)
CORNER = ((4, 3, 8, 128), F32)
RIMS = [FACE, FACE, SIDE, SIDE]
SLOTS = ((128, 4, 128), F32)
MESH = pl.DeviceIdType.MESH
LIMIT = 40 * 1024 * 1024


def rim_copies(n_ax, n_xs, sent, landed, corners, send_sems, recv_sems):
    ax, xs = lax.axis_index("ax"), lax.axis_index("xs")
    low, high, left, right = sent
    plan = [
        (high, landed[0], 1, 0),
        (low, landed[1], -1, 0),
        (right, landed[2], 0, 1),
        (left, landed[3], 0, -1),
        (right.at[:, 1, 1], corners.at[0], 1, 1),
        (right.at[:, 0, 0], corners.at[1], -1, 1),
        (left.at[:, 1, 1], corners.at[2], 1, -1),
        (left.at[:, 0, 0], corners.at[3], -1, -1),
    ]
    return [
        pltpu.make_async_remote_copy(
            src_ref=src,
            dst_ref=dst,
            send_sem=send_sems.at[n],
            recv_sem=recv_sems.at[n],
            device_id=(lax.rem(ax + da + n_ax, n_ax), lax.rem(xs + dx + n_xs, n_xs)),
            device_id_type=MESH,
        )
        for n, (src, dst, da, dx) in enumerate(plan)
    ]


def main_body(n_ax, n_xs, *refs):
    sources = refs[:11]
    turned, cnew, snew = refs[11:14]
    held = refs[14:25]
    (idx, off, own, piece, flow, heat, stiff, inert, share, freq, energy) = held
    (rank, pay, got, back, ret, x, h, g, c, table, lag, halves, probe, coords) = refs[25:39]
    (low1, high1, left1, right1, low2, high2, left2, right2, corners1) = refs[39:48]
    (low3, high3, left3, right3, low4, high4, left4, right4, corners2) = refs[48:57]
    (in_sems, out_send, out_recv, back_send, back_recv, rim_send, rim_recv) = refs[57:]
    devices = n_ax * n_xs
    ax, xs = lax.axis_index("ax"), lax.axis_index("xs")
    me = ax * n_xs + xs

    loads = [
        pltpu.make_async_copy(src, dst, in_sems.at[n])
        for n, (src, dst) in enumerate(zip(sources, held))
    ]
    for load in loads:
        load.start()

    def where(n):
        return (lax.div(n, n_xs), lax.rem(n, n_xs))

    barrier = pltpu.get_barrier_semaphore()

    def greet(k, carry):
        pl.semaphore_signal(
            barrier, inc=1, device_id=where(lax.rem(me + k, devices)), device_id_type=MESH
        )
        return carry

    lax.fori_loop(1, devices, greet, 0)
    for load in loads[:4]:
        load.wait()
    dispatch(idx, off, own, piece, coords, rank, pay)
    for load in loads[4:]:
        load.wait()
    turn_in(flow, heat, stiff, inert, x, table, g, c)
    pl.semaphore_wait(barrier, devices - 1)

    own_copy = pltpu.make_async_copy(pay.at[me], got.at[me], out_recv.at[ax])
    own_copy.start()

    def send_to(row, column):
        pltpu.make_async_remote_copy(
            src_ref=pay.at[row * n_xs + column],
            dst_ref=got.at[me],
            send_sem=out_send,
            recv_sem=out_recv.at[ax],
            device_id=(row, column),
            device_id_type=MESH,
        ).start()

    for dx in range(1, n_xs):
        send_to(ax, lax.rem(xs + dx, n_xs))

    def send(da, carry):
        row = lax.rem(ax + da, n_ax)
        for dx in range(n_xs):
            send_to(row, lax.rem(xs + dx, n_xs))
        return carry

    lax.fori_loop(1, n_ax, send, 0)

    helm(x, g, c, h)
    faces(h, low1, high1, left1, right1)
    first = rim_copies(
        n_ax, n_xs, (low1, high1, left1, right1), (low2, high2, left2, right2), corners1,
        rim_send.at[0], rim_recv.at[0],
    )
    for copy in first:
        copy.start()

    def block(n, carry):
        now = lax.rem(ax + 2 * n_ax - 1 - n, n_ax)
        base = now * n_xs
        rows = got.at[pl.ds(base, n_xs)]
        pltpu.make_async_copy(rows, rows, out_recv.at[now]).wait()
        for part in range(n_xs // 8):
            interpolate(base + part * 8, got, table, back, lag.at[part])

        def give(to, row, column):
            pltpu.make_async_remote_copy(
                src_ref=back.at[to],
                dst_ref=ret.at[me],
                send_sem=back_send,
                recv_sem=back_recv,
                device_id=(row, column),
                device_id_type=MESH,
            ).start()

        @pl.when(now != ax)
        def _():
            for column in range(n_xs):
                give(base + column, now, column)

        @pl.when(now == ax)
        def _():
            for step in range(1, n_xs):
                column = lax.rem(xs + step, n_xs)
                give(base + column, ax, column)
            pltpu.make_async_copy(back.at[me], ret.at[me], back_recv).start()

        return carry

    lax.fori_loop(0, n_ax // 4, block, 0)
    for copy in first:
        copy.wait()
    assemble(h, low2, high2, left2, right2, corners1, ax == 0, ax == n_ax - 1)
    helm(h, g, c, x)
    faces(x, low3, high3, left3, right3)
    second = rim_copies(
        n_ax, n_xs, (low3, high3, left3, right3), (low4, high4, left4, right4), corners2,
        rim_send.at[1], rim_recv.at[1],
    )
    for copy in second:
        copy.start()
    lax.fori_loop(n_ax // 4, n_ax, block, 0)

    for copy in second:
        copy.wait()
    assemble(x, low4, high4, left4, right4, corners2, ax == 0, ax == n_ax - 1)
    turn_out(x, turned)
    pltpu.make_async_copy(ret, ret, back_recv).wait()
    gather_back(ret, own, rank, probe, halves)
    kinetics(probe, coords, share, freq, energy, cnew, snew)

    others = pl.ds(0, devices - 1)
    pltpu.make_async_copy(pay.at[others], pay.at[others], out_send).wait()
    pltpu.make_async_copy(back.at[others], back.at[others], back_send).wait()


def last_body(*refs):
    copies = [pltpu.make_async_copy(refs[n], refs[3 + n], refs[6].at[n]) for n in range(3)]
    for copy in copies:
        copy.start()
    for copy in copies:
        copy.wait()


def shapes(outs):
    return [jax.ShapeDtypeStruct(shape, dtype) for shape, dtype in outs]


def buffers(outs):
    return [pltpu.VMEM(shape, dtype) for shape, dtype in outs]


def local(flow, heat, stiff, inert, index, offset, owner, piece, shares, freq, barrier):
    particles = piece.shape[0]
    n_ax, n_xs = lax.axis_size("ax"), lax.axis_size("xs")
    devices = n_ax * n_xs
    vmem = pl.BlockSpec(memory_space=pltpu.VMEM)
    hbm = pl.BlockSpec(memory_space=pltpu.HBM)
    inputs = (
        index,
        offset,
        owner.reshape(1, particles),
        piece.reshape(1, particles),
        flow.reshape(3, 256, 512),
        heat.reshape(256, 512),
        stiff.reshape(3, 256, 512),
        inert.reshape(256, 512),
        shares,
        freq,
        barrier,
    )
    inputs = [pltpu.with_memory_space_constraint(a, pltpu.HBM) for a in inputs]
    held = [(a.shape, a.dtype) for a in inputs]
    table = ((2048, 256), BF16)
    outs = [((3, 256, 512), F32), ((3, particles), F32), ((6, particles), F32)]
    passed = pl.pallas_call(
        functools.partial(main_body, n_ax, n_xs),
        out_shape=shapes(outs),
        in_specs=[hbm] * 11,
        out_specs=[vmem] * len(outs),
        scratch_shapes=buffers(held[:9])
        + [pltpu.SMEM(*one) for one in held[9:]]
        + buffers([((1, particles), jnp.int32), SLOTS, SLOTS, SLOTS, SLOTS, FIELD, FIELD, FIELD])
        + buffers([((2, 512, 128), F32), table, ((2, 192, 128), F32), ((512, 256), BF16)])
        + buffers([((4, particles), F32), ((3, particles), F32)])
        + buffers([*RIMS, *RIMS, CORNER, *RIMS, *RIMS, CORNER])
        + [
            pltpu.SemaphoreType.DMA((11,)),
            pltpu.SemaphoreType.DMA,
            pltpu.SemaphoreType.DMA((n_ax,)),
            pltpu.SemaphoreType.DMA,
            pltpu.SemaphoreType.DMA,
            pltpu.SemaphoreType.DMA((2, 8)),
            pltpu.SemaphoreType.DMA((2, 8)),
        ],
        compiler_params=pltpu.CompilerParams(
            collective_id=0, has_side_effects=True, vmem_limit_bytes=LIMIT
        ),
    )(*inputs)
    out, cnew, snew = pl.pallas_call(
        last_body,
        out_shape=shapes(outs),
        in_specs=[vmem] * 3,
        out_specs=[hbm] * 3,
        scratch_shapes=[pltpu.SemaphoreType.DMA((3,))],
        compiler_params=pltpu.CompilerParams(vmem_limit_bytes=8 * 1024 * 1024),
    )(*passed)
    return out.reshape(flow.shape), cnew, snew


def solution(mesh):
    placed = (
        P(None, "ax", "xs", None, None),
        P("ax", "xs", None, None),
        P(None, "ax", "xs", None, None),
        P("ax", "xs", None, None),
        P(None, ("ax", "xs")),
        P(None, ("ax", "xs")),
        P(("ax", "xs"), None),
        P(("ax", "xs")),
        P(None, ("ax", "xs")),
        P(),
        P(),
    )
    return jax.shard_map(
        local,
        mesh=mesh,
        in_specs=placed,
        out_specs=(P(None, "ax", "xs", None, None), P(None, ("ax", "xs")), P(None, ("ax", "xs"))),
        check_vma=False,
    )
```

```python
import functools

import jax
import jax.numpy as jnp
import numpy as np
from jax import lax
from jax.experimental import pallas as pl
from jax.experimental.pallas import tpu as pltpu
from jax.sharding import PartitionSpec as P

NODE_LIST = (
    -1.0,
    -0.8717401485096066,
    -0.5917001814331423,
    -0.2092992179024789,
    0.2092992179024789,
    0.5917001814331423,
    0.8717401485096066,
    1.0,
)
STEP_DT = 0.25
F32 = jnp.float32
BF16 = jnp.bfloat16
CHUNK = 256


def bary_weights():
    nodes = np.array(NODE_LIST)
    weights = np.zeros(8)
    for a in range(8):
        weights[a] = 1.0 / np.prod([nodes[a] - nodes[m] for m in range(8) if m != a])
    return nodes, weights


def deriv_table():
    nodes, weights = bary_weights()
    table = np.zeros((8, 8))
    for row in range(8):
        for col in range(8):
            if row != col:
                table[row, col] = weights[col] / weights[row] / (nodes[row] - nodes[col])
        table[row, row] = -np.sum(table[row])
    return table


DM = np.asarray(deriv_table(), np.float32).astype(np.float64)


def apply_table(table, u):
    even = [u[i] + u[7 - i] for i in range(4)]
    odd = [u[i] - u[7 - i] for i in range(4)]
    out = [None] * 8
    for p in range(4):
        a = b = None
        for i in range(4):
            ca = float((table[p, i] + table[p, 7 - i]) / 2)
            cb = float((table[p, i] - table[p, 7 - i]) / 2)
            ta, tb = even[i] * ca, odd[i] * cb
            a = ta if a is None else a + ta
            b = tb if b is None else b + tb
        out[p], out[7 - p] = a + b, b - a
    return out


def pick_node(cell, shift):
    out = jnp.full(cell.shape, NODE_LIST[shift], F32)
    for c in range(1, 7):
        out = jnp.where(cell == c, F32(NODE_LIST[c + shift]), out)
    return out


def split(x):
    high = x.astype(BF16).astype(F32)
    return high, x - high


def dispatch(idx_ref, off_ref, own_ref, piece_ref, coords_ref, rank_ref, pay_ref):
    total = idx_ref.shape[1]
    cell = idx_ref[...]
    low, high = pick_node(cell, 0), pick_node(cell, 1)
    coords_ref[...] = low + off_ref[...] * (high - low)
    rows = lax.broadcasted_iota(jnp.int32, (CHUNK, 2 * CHUNK), 0)
    cols = lax.broadcasted_iota(jnp.int32, (CHUNK, 2 * CHUNK), 1)
    before = jnp.where((rows < cols) | (cols >= CHUNK), 1.0, 0.0).astype(BF16)
    lane_id = lax.broadcasted_iota(jnp.int32, (128, CHUNK), 0)
    base = jnp.zeros((128, CHUNK), F32)
    for c in range(total // CHUNK):
        part = pl.ds(c * CHUNK, CHUNK)
        hot = jnp.where(own_ref[:, part] == lane_id, 1.0, 0.0)
        count = jnp.dot(hot.astype(BF16), before, preferred_element_type=F32)
        rank = jnp.sum(hot * (count[:, :CHUNK] + base), axis=0, keepdims=True)
        rank_ref[:, part] = rank.astype(jnp.int32)
        base = base + count[:, CHUNK:]
    sums = [jnp.zeros((128, 128), F32)] * 4
    dims = (((1,), (1,)), ((), ()))
    for c in range(total // CHUNK):
        part = pl.ds(c * CHUNK, CHUNK)
        hot = jnp.where(own_ref[:, part] == lane_id, 1.0, 0.0).astype(BF16)
        mask = rank_ref[:, part] == lane_id
        tops, lows = [], []
        for d in range(3):
            high, rest = split(coords_ref[pl.ds(d, 1), part])
            tops.append(jnp.where(mask, high, 0.0).astype(BF16))
            lows.append(jnp.where(mask, rest, 0.0).astype(BF16))
        tops.append(jnp.where(mask, piece_ref[:, part].astype(F32), 0.0).astype(BF16))
        one = lax.dot_general(hot, jnp.concatenate(tops, 0), dims, preferred_element_type=F32)
        two = lax.dot_general(hot, jnp.concatenate(lows, 0), dims, preferred_element_type=F32)
        sums = [
            sums[v] + (one[:, v * 128 : (v + 1) * 128] + two[:, v * 128 : (v + 1) * 128] if v < 3 else one[:, 384:])
            for v in range(4)
        ]
    for v in range(4):
        pay_ref[:, v, :] = sums[v]


def interpolate(base, got_ref, table_ref, back_ref, lag_ref):
    nodes, weights = bary_weights()
    ident = lax.broadcasted_iota(jnp.int32, (256, 256), 0)
    for d in range(3):
        x = got_ref[pl.ds(base, 8), d, :]
        diff = [x - F32(n) for n in nodes]
        ahead, behind = [None] * 8, [None] * 8
        ahead[1], behind[6] = diff[0], diff[7]
        for i in range(2, 8):
            ahead[i] = ahead[i - 1] * diff[i - 1]
            behind[7 - i] = behind[8 - i] * diff[8 - i]
        for i in range(8):
            prod = behind[0] if i == 0 else ahead[7] if i == 7 else ahead[i] * behind[i]
            lag_ref[pl.ds(d * 64 + i * 8, 8), :] = prod * F32(weights[i])
    elem = got_ref[pl.ds(base, 8), 3, :].astype(jnp.int32)
    for pair in range(4):
        s0, s1 = 2 * pair, 2 * pair + 1
        ids = jnp.concatenate([elem[s0 : s0 + 1], elem[s1 : s1 + 1]], 1)
        hot = jnp.where(ident == ids, 1.0, 0.0).astype(BF16)

        def weight(d, i):
            row = d * 64 + i * 8
            return jnp.concatenate(
                [lag_ref[pl.ds(row + s0, 1), :], lag_ref[pl.ds(row + s1, 1), :]], 1
            )

        third = jnp.concatenate(
            [lag_ref[pl.ds(128 + s0, 8, stride=8), :], lag_ref[pl.ds(128 + s1, 8, stride=8), :]], 1
        )
        rows = jnp.dot(table_ref[...], hot, preferred_element_type=F32)
        for f in range(4):
            one = None
            for i in range(8):
                at = f * 512 + i * 64
                term = rows[at : at + 64] * weight(0, i)
                one = term if one is None else one + term
            two = None
            for j in range(8):
                term = one[j * 8 : (j + 1) * 8] * weight(1, j)
                two = term if two is None else two + term
            value = jnp.sum(two * third, axis=0, keepdims=True)
            back_ref[base + s0, pl.ds(f, 1), :] = value[:, :128]
            back_ref[base + s1, pl.ds(f, 1), :] = value[:, 128:]


def gather_back(ret_ref, own_ref, rank_ref, probe_ref, halves_ref):
    total = own_ref.shape[1]
    for f in range(4):
        high, rest = split(jnp.transpose(ret_ref[:, f, :]))
        halves_ref[pl.ds(f * 128, 128), 0:128] = high.astype(BF16)
        halves_ref[pl.ds(f * 128, 128), 128:256] = rest.astype(BF16)
    lane_id = lax.broadcasted_iota(jnp.int32, (128, CHUNK), 0)
    for c in range(total // CHUNK):
        part = pl.ds(c * CHUNK, CHUNK)
        hot = jnp.where(own_ref[:, part] == lane_id, 1.0, 0.0).astype(BF16)
        found = jnp.dot(
            halves_ref[...], jnp.concatenate([hot, hot], 0), preferred_element_type=F32
        )
        mask = rank_ref[:, part] == lane_id
        for f in range(4):
            kept = jnp.where(mask, found[f * 128 : (f + 1) * 128], 0.0)
            probe_ref[pl.ds(f, 1), part] = jnp.sum(kept, axis=0, keepdims=True)


def kinetics(probe_ref, coords_ref, share_ref, freq_ref, barrier_ref, cnew_ref, snew_ref):
    cnew_ref[...] = coords_ref[...] + STEP_DT * probe_ref[0:3, :]
    shares = share_ref[...]
    species = lax.broadcasted_iota(jnp.int32, shares.shape, 0)
    freq = jnp.full(shares.shape, freq_ref[0], F32)
    barrier = jnp.full(shares.shape, barrier_ref[0], F32)
    for q in range(1, 6):
        freq = jnp.where(species == q, freq_ref[q], freq)
        barrier = jnp.where(species == q, barrier_ref[q], barrier)
    rates = freq * jnp.exp(barrier * jnp.tanh(probe_ref[3:4, :] - 1.0))
    flux = rates * shares
    moved = jnp.concatenate([flux[5:6], flux[0:5]], 0)
    snew_ref[...] = shares + STEP_DT * (moved - flux)


def turn_in(flow_ref, heat_ref, stiff_ref, inert_ref, x_ref, table_ref, g_ref, c_ref):
    def three(d, carry):
        for a in range(2):
            lanes = pl.ds(a * 128, 128)
            turned = jnp.transpose(flow_ref[d, lanes, :].astype(F32))
            x_ref[d * 2 + a] = turned
            table_ref[pl.ds(pl.multiple_of(d * 512, 512), 512), lanes] = turned.astype(BF16)
            g_ref[d * 2 + a] = jnp.transpose(stiff_ref[d, lanes, :])
        return carry

    lax.fori_loop(0, 3, three, 0)
    for a in range(2):
        lanes = pl.ds(a * 128, 128)
        table_ref[pl.ds(1536, 512), lanes] = jnp.transpose(heat_ref[lanes, :].astype(F32)).astype(BF16)
        c_ref[a] = jnp.transpose(inert_ref[lanes, :])


def helm(x_ref, g_ref, c_ref, h_ref):
    def part(n, carry):
        a = n % 2

        def along(d, at):
            line = apply_table(DM, [x_ref[n, p, :] for p in at])
            return apply_table(DM.T, [g_ref[d * 2 + a, at[p], :] * line[p] for p in range(8)])

        for i in range(8):
            at = [pl.ds(i * 64 + j * 8, 8) for j in range(8)]
            line = along(1, at)
            for j in range(8):
                h_ref[n, at[j], :] = line[j] + c_ref[a, at[j], :] * x_ref[n, at[j], :]
        for j in range(8):
            at = [pl.ds(i * 64 + j * 8, 8) for i in range(8)]
            line = along(0, at)
            for i in range(8):
                h_ref[n, at[i], :] += line[i]
        for i in range(8):
            at = [pl.ds(i * 64 + k, 8, stride=8) for k in range(8)]
            line = along(2, at)
            for k in range(8):
                h_ref[n, at[k], :] += line[k]
        return carry

    lax.fori_loop(0, 6, part, 0)


def faces(h_ref, low_ref, high_ref, left_ref, right_ref):
    for f in range(3):
        low_ref[f] = h_ref[2 * f, 0:64]
        high_ref[f] = h_ref[2 * f + 1, 448:512]
        both = h_ref[2 * f, 448:512] + h_ref[2 * f + 1, 0:64]
        h_ref[2 * f, 448:512] = both
        h_ref[2 * f + 1, 0:64] = both
    lane = lax.broadcasted_iota(jnp.int32, (8, 128), 1) // 32

    def pack(n, carry):
        f, a = n // 2, n % 2
        for half in range(2):
            one = two = None
            for q in range(4):
                row = (half * 4 + q) * 64
                first = h_ref[n, pl.ds(row, 8), :]
                last = h_ref[n, pl.ds(row + 56, 8), :]
                if q:
                    first = pltpu.roll(first, 32 * q, 1)
                if q < 3:
                    last = pltpu.roll(last, 32 * q + 32, 1)
                one = first if one is None else jnp.where(lane == q, first, one)
                two = last if two is None else jnp.where(lane == q, last, two)
            left_ref[f, a, half] = one
            right_ref[f, a, half] = two
        return carry

    lax.fori_loop(0, 6, pack, 0)


def assemble(h_ref, low_ref, high_ref, left_ref, right_ref, corner_ref):
    lane = lax.broadcasted_iota(jnp.int32, (8, 128), 1)
    quarter, radial = lane // 32, lane % 32

    def near(f, carry):
        def corner(n, q, turn):
            return jnp.where(quarter == q, pltpu.roll(corner_ref[n, f], turn, 1), 0.0)

        h_ref[2 * f, 0:64] += low_ref[f]
        h_ref[2 * f + 1, 448:512] += high_ref[f]
        left_ref[f, 0, 0] += corner(0, 0, 32)
        left_ref[f, 1, 1] += corner(1, 3, 96)
        right_ref[f, 0, 0] += corner(2, 0, 32)
        right_ref[f, 1, 1] += corner(3, 3, 96)
        return carry

    lax.fori_loop(0, 3, near, 0)

    def part(n, carry):
        f, a = n // 2, n % 2
        for i in range(8):
            half, q = i // 4, i % 4
            first = h_ref[n, pl.ds(i * 64, 8), :]
            last = h_ref[n, pl.ds(i * 64 + 56, 8), :]
            before, after = left_ref[f, a, half], right_ref[f, a, half]
            if q:
                before = pltpu.roll(before, 128 - 32 * q, 1)
            if q < 3:
                after = pltpu.roll(after, 96 - 32 * q, 1)
            before = jnp.where(quarter == 0, before, pltpu.roll(last, 32, 1))
            after = jnp.where(quarter == 3, after, pltpu.roll(first, 96, 1))
            h_ref[n, pl.ds(i * 64, 8), :] = first + before
            h_ref[n, pl.ds(i * 64 + 56, 8), :] = last + after
        for i in range(8):
            inner, outer = pl.ds(i * 64, 8, stride=8), pl.ds(i * 64 + 7, 8, stride=8)
            first, last = h_ref[n, inner, :], h_ref[n, outer, :]
            h_ref[n, inner, :] = first + jnp.where(radial != 0, pltpu.roll(last, 1, 1), 0.0)
            h_ref[n, outer, :] = last + jnp.where(radial != 31, pltpu.roll(first, 127, 1), 0.0)
        return carry

    lax.fori_loop(0, 6, part, 0)


def turn_out(x_ref, out_ref):
    def three(d, carry):
        for a in range(2):
            lanes = pl.ds(a * 128, 128)
            out_ref[d, lanes, :] = jnp.transpose(x_ref[d * 2 + a])
        return carry

    lax.fori_loop(0, 3, three, 0)


FIELD = ((6, 512, 128), F32)
FACE = ((3, 64, 128), F32)
SIDE = ((3, 2, 2, 8, 128), F32)
CORNER = ((4, 3, 8, 128), F32)
RIMS = [FACE, FACE, SIDE, SIDE]
SLOTS = ((128, 4, 128), F32)
MESH = pl.DeviceIdType.MESH
LIMIT = 40 * 1024 * 1024


def rim_copies(n_ax, n_xs, sent, landed, corners, send_sems, recv_sems):
    ax, xs = lax.axis_index("ax"), lax.axis_index("xs")
    low, high, left, right = sent
    plan = [
        (high, landed[0], 1, 0),
        (low, landed[1], -1, 0),
        (right, landed[2], 0, 1),
        (left, landed[3], 0, -1),
        (right.at[:, 1, 1], corners.at[0], 1, 1),
        (right.at[:, 0, 0], corners.at[1], -1, 1),
        (left.at[:, 1, 1], corners.at[2], 1, -1),
        (left.at[:, 0, 0], corners.at[3], -1, -1),
    ]
    copies = [
        pltpu.make_async_remote_copy(
            src_ref=src,
            dst_ref=dst,
            send_sem=send_sems.at[n],
            recv_sem=recv_sems.at[n],
            device_id=(lax.rem(ax + da + n_ax, n_ax), lax.rem(xs + dx + n_xs, n_xs)),
            device_id_type=MESH,
        )
        for n, (src, dst, da, dx) in enumerate(plan)
    ]
    below, above = ax > 0, ax < n_ax - 1

    def each(da, there, action):
        if da == 0:
            action()
        else:
            pl.when(above if da == there else below)(action)

    def start():
        for copy, (_, _, da, _) in zip(copies, plan):
            each(da, 1, copy.start)

    def wait():
        for copy, (_, _, da, _) in zip(copies, plan):
            each(da, 1, copy.wait_send)
            each(da, -1, copy.wait_recv)

    return start, wait


def main_body(n_ax, n_xs, *refs):
    sources = refs[:11]
    turned, cnew, snew = refs[11:14]
    held = refs[14:25]
    (idx, off, own, piece, flow, heat, stiff, inert, share, freq, energy) = held
    (rank, pay, got, back, ret, x, h, g, c, table, lag, halves, probe, coords) = refs[25:39]
    (low1, high1, left1, right1, low2, high2, left2, right2, corners1) = refs[39:48]
    (low3, high3, left3, right3, low4, high4, left4, right4, corners2) = refs[48:57]
    (in_sems, out_send, out_recv, back_send, back_recv, rim_send, rim_recv) = refs[57:]
    devices = n_ax * n_xs
    ax, xs = lax.axis_index("ax"), lax.axis_index("xs")
    me = ax * n_xs + xs

    loads = [
        pltpu.make_async_copy(src, dst, in_sems.at[n])
        for n, (src, dst) in enumerate(zip(sources, held))
    ]
    for load in loads:
        load.start()

    def where(n):
        return (lax.div(n, n_xs), lax.rem(n, n_xs))

    barrier = pltpu.get_barrier_semaphore()

    def greet(k, carry):
        pl.semaphore_signal(
            barrier, inc=1, device_id=where(lax.rem(me + k, devices)), device_id_type=MESH
        )
        return carry

    lax.fori_loop(1, devices, greet, 0)

    @pl.when(ax == 0)
    def _():
        for low, corners in ((low2, corners1), (low4, corners2)):
            low[...] = jnp.zeros_like(low)
            corners[0] = jnp.zeros((3, 8, 128), F32)
            corners[2] = jnp.zeros((3, 8, 128), F32)

    @pl.when(ax == n_ax - 1)
    def _():
        for high, corners in ((high2, corners1), (high4, corners2)):
            high[...] = jnp.zeros_like(high)
            corners[1] = jnp.zeros((3, 8, 128), F32)
            corners[3] = jnp.zeros((3, 8, 128), F32)

    for load in loads[:4]:
        load.wait()
    dispatch(idx, off, own, piece, coords, rank, pay)
    for load in loads[4:]:
        load.wait()
    turn_in(flow, heat, stiff, inert, x, table, g, c)
    pl.semaphore_wait(barrier, devices - 1)

    own_copy = pltpu.make_async_copy(pay.at[me], got.at[me], out_recv.at[ax])
    own_copy.start()

    def send_to(row, column):
        pltpu.make_async_remote_copy(
            src_ref=pay.at[row * n_xs + column],
            dst_ref=got.at[me],
            send_sem=out_send,
            recv_sem=out_recv.at[ax],
            device_id=(row, column),
            device_id_type=MESH,
        ).start()

    def send(da, carry):
        row = lax.rem(ax + n_ax - da, n_ax)
        for dx in range(n_xs):
            send_to(row, lax.rem(xs + dx, n_xs))
        return carry

    lax.fori_loop(1, n_ax, send, 0)
    for dx in range(1, n_xs):
        send_to(ax, lax.rem(xs + dx, n_xs))

    helm(x, g, c, h)
    faces(h, low1, high1, left1, right1)
    first = rim_copies(
        n_ax, n_xs, (low1, high1, left1, right1), (low2, high2, left2, right2), corners1,
        rim_send.at[0], rim_recv.at[0],
    )
    first[0]()

    def block(n, carry):
        now = lax.rem(ax + 1 + n, n_ax)
        base = now * n_xs
        rows = got.at[pl.ds(base, n_xs)]
        pltpu.make_async_copy(rows, rows, out_recv.at[now]).wait()
        for part in range(n_xs // 8):
            interpolate(base + part * 8, got, table, back, lag.at[part])

        def give(to, row, column):
            pltpu.make_async_remote_copy(
                src_ref=back.at[to],
                dst_ref=ret.at[me],
                send_sem=back_send,
                recv_sem=back_recv,
                device_id=(row, column),
                device_id_type=MESH,
            ).start()

        @pl.when(now != ax)
        def _():
            for column in range(n_xs):
                give(base + column, now, column)

        @pl.when(now == ax)
        def _():
            for step in range(1, n_xs):
                column = lax.rem(xs + step, n_xs)
                give(base + column, ax, column)
            pltpu.make_async_copy(back.at[me], ret.at[me], back_recv).start()

        return carry

    lax.fori_loop(0, n_ax // 4, block, 0)
    first[1]()
    assemble(h, low2, high2, left2, right2, corners1)
    helm(h, g, c, x)
    faces(x, low3, high3, left3, right3)
    second = rim_copies(
        n_ax, n_xs, (low3, high3, left3, right3), (low4, high4, left4, right4), corners2,
        rim_send.at[1], rim_recv.at[1],
    )
    second[0]()
    lax.fori_loop(n_ax // 4, n_ax, block, 0)

    second[1]()
    assemble(x, low4, high4, left4, right4, corners2)
    turn_out(x, turned)
    pltpu.make_async_copy(ret, ret, back_recv).wait()
    gather_back(ret, own, rank, probe, halves)
    kinetics(probe, coords, share, freq, energy, cnew, snew)

    others = pl.ds(0, devices - 1)
    pltpu.make_async_copy(pay.at[others], pay.at[others], out_send).wait()
    pltpu.make_async_copy(back.at[others], back.at[others], back_send).wait()


def last_body(*refs):
    copies = [pltpu.make_async_copy(refs[n], refs[3 + n], refs[6].at[n]) for n in range(3)]
    for copy in copies:
        copy.start()
    for copy in copies:
        copy.wait()


def shapes(outs):
    return [jax.ShapeDtypeStruct(shape, dtype) for shape, dtype in outs]


def buffers(outs):
    return [pltpu.VMEM(shape, dtype) for shape, dtype in outs]


def local(flow, heat, stiff, inert, index, offset, owner, piece, shares, freq, barrier):
    particles = piece.shape[0]
    n_ax, n_xs = lax.axis_size("ax"), lax.axis_size("xs")
    devices = n_ax * n_xs
    vmem = pl.BlockSpec(memory_space=pltpu.VMEM)
    hbm = pl.BlockSpec(memory_space=pltpu.HBM)
    inputs = (
        index,
        offset,
        owner.reshape(1, particles),
        piece.reshape(1, particles),
        flow.reshape(3, 256, 512),
        heat.reshape(256, 512),
        stiff.reshape(3, 256, 512),
        inert.reshape(256, 512),
        shares,
        freq,
        barrier,
    )
    inputs = [pltpu.with_memory_space_constraint(a, pltpu.HBM) for a in inputs]
    held = [(a.shape, a.dtype) for a in inputs]
    table = ((2048, 256), BF16)
    outs = [((3, 256, 512), F32), ((3, particles), F32), ((6, particles), F32)]
    passed = pl.pallas_call(
        functools.partial(main_body, n_ax, n_xs),
        out_shape=shapes(outs),
        in_specs=[hbm] * 11,
        out_specs=[vmem] * len(outs),
        scratch_shapes=buffers(held[:9])
        + [pltpu.SMEM(*one) for one in held[9:]]
        + buffers([((1, particles), jnp.int32), SLOTS, SLOTS, SLOTS, SLOTS, FIELD, FIELD, FIELD])
        + buffers([((2, 512, 128), F32), table, ((2, 192, 128), F32), ((512, 256), BF16)])
        + buffers([((4, particles), F32), ((3, particles), F32)])
        + buffers([*RIMS, *RIMS, CORNER, *RIMS, *RIMS, CORNER])
        + [
            pltpu.SemaphoreType.DMA((11,)),
            pltpu.SemaphoreType.DMA,
            pltpu.SemaphoreType.DMA((n_ax,)),
            pltpu.SemaphoreType.DMA,
            pltpu.SemaphoreType.DMA,
            pltpu.SemaphoreType.DMA((2, 8)),
            pltpu.SemaphoreType.DMA((2, 8)),
        ],
        compiler_params=pltpu.CompilerParams(
            collective_id=0, has_side_effects=True, vmem_limit_bytes=LIMIT
        ),
    )(*inputs)
    out, cnew, snew = pl.pallas_call(
        last_body,
        out_shape=shapes(outs),
        in_specs=[vmem] * 3,
        out_specs=[hbm] * 3,
        scratch_shapes=[pltpu.SemaphoreType.DMA((3,))],
        compiler_params=pltpu.CompilerParams(vmem_limit_bytes=8 * 1024 * 1024),
    )(*passed)
    return out.reshape(flow.shape), cnew, snew


def solution(mesh):
    placed = (
        P(None, "ax", "xs", None, None),
        P("ax", "xs", None, None),
        P(None, "ax", "xs", None, None),
        P("ax", "xs", None, None),
        P(None, ("ax", "xs")),
        P(None, ("ax", "xs")),
        P(("ax", "xs"), None),
        P(("ax", "xs")),
        P(None, ("ax", "xs")),
        P(),
        P(),
    )
    return jax.shard_map(
        local,
        mesh=mesh,
        in_specs=placed,
        out_specs=(P(None, "ax", "xs", None, None), P(None, ("ax", "xs")), P(None, ("ax", "xs"))),
        check_vma=False,
    )
```
